512 devices in a mesh: band: 64 (over z, y), lev: 8 (over x, core).
Axes of the slice: x: 4, y: 8, z: 8, core: 2. Of those that a mesh axis runs over, the one named last changes fastest.
Arguments:
- spectra: bfloat16 [2, 64, 320, 641], P(None, 'lev', 'band'), may hold values from -0.15625 to 0.15625
- legendre: bfloat16 [8, 64, 320, 641], P('lev', None, 'band'), may hold values from -0.25 to 0.25
- pairing: int32 [320], P('band'), may hold values from 0 to 319, each once
- eta_shift: bfloat16 [16, 512, 2816], P('lev', 'band'), may hold values from -4 to 4
- cells: int32 [3, 16, 512, 2816], P(None, 'lev', 'band'), may hold values from -1 to 2815, as said below
Outputs:
- advected: bfloat16 [2, 16, 512, 2816], P(None, 'lev', 'band')
- displacement: float32 [2, 16, 512, 2816], P(None, 'lev', 'band')
The draws below stay inside these ranges and needn't reach their ends.
Inputs may be any that keep to these rules, and one draw needn't show every extreme that they name: cells[0] is the arrival row or the row before it, cells[1] the arrival longitude or the one before it (cyclically), cells[2] the arrival level or the one before it.
All inputs are finite; a program needn't handle non-finite values.
Results may differ from the reference program's by a relative error of at most 0.0076.
Values may be sent and summed in bfloat16 or wider, within the bound.
A program may use at most 64 MiB of HBM per device.

```python
import math
import jax
import jax.numpy as jnp
from jax import lax

M = 640
NLON = 2816
LEV = 16
ITERS = 2
LAT_DEV = 8
LAT = 512
PAIRS = 320
N_BAND = 64


def draw_cells(key, part):
    key = jax.random.fold_in(key, 7)
    key_row, key_lon, key_level = jax.random.split(key, 3)
    grid_shape = (LEV, LAT, NLON)
    row_cells = lax.broadcasted_iota(jnp.int32, grid_shape, 1) - jax.random.randint(key_row, grid_shape, 0, 2)
    lon_cells = (lax.broadcasted_iota(jnp.int32, grid_shape, 2) - jax.random.randint(key_lon, grid_shape, 0, 2)) % NLON
    level_cells = lax.broadcasted_iota(jnp.int32, grid_shape, 0) - jax.random.randint(key_level, grid_shape, 0, 2)
    return jnp.stack([row_cells, lon_cells, level_cells]).astype(jnp.int32)


def levels(key, shape, shards, least, top_value):
    def one(dim, parts):
        heights = jax.random.uniform(jax.random.fold_in(jax.random.fold_in(key, 6), dim), (parts,), jnp.float32, least / len(shards), top_value / len(shards))
        return jnp.repeat(jnp.exp(heights), shape[dim] // parts).reshape((-1,) + (1,) * (len(shape) - dim - 1))

    gain = one(*shards[0])
    for cut in shards[1:]:
        gain = gain * one(*cut)
    return gain


def bell_draw(rng, shape, scale, limit, cuts=(), kind=jnp.bfloat16):
    drawn = jax.random.normal(rng, shape, jnp.float32) * scale
    if len(cuts) > 0:
        drawn = levels(rng, shape, cuts, -0.22, 0.18) * drawn
    return jnp.clip(drawn, min=-limit, max=limit).astype(kind)


def setup_inputs(seed: int = 0) -> dict:
    key_list = jax.random.split(jax.random.key(seed), 6)
    spectra = bell_draw(key_list[0], (2, 4 * LEV, PAIRS, M + 1), ((2 * M) ** -0.5), 0.15625, ((1, 8), (2, 64)))
    legendre = bell_draw(key_list[1], (LAT_DEV, N_BAND, PAIRS, M + 1), (M + 1) ** -0.5, 0.25, ((0, 8), (2, 64)))
    pairing = jax.random.permutation(key_list[2], PAIRS).astype(jnp.int32)
    eta_shift = bell_draw(key_list[3], (LEV, LAT, NLON), 0.6, 4.0, ((0, 8), (1, 64)))
    cells = draw_cells(jax.random.fold_in(key_list[5], 71), 0)
    return {"spectra": spectra, "legendre": legendre, "pairing": pairing, "eta_shift": eta_shift, "cells": cells}


COURANT = 0.8


def cubic_weights(fraction):
    return (-fraction * (fraction - 1.0) * (fraction - 2.0) / 6.0,
            (fraction + 1.0) * (fraction - 1.0) * (fraction - 2.0) / 2.0,
            -(fraction + 1.0) * fraction * (fraction - 2.0) / 2.0,
            (fraction + 1.0) * fraction * (fraction - 1.0) / 6.0)


def tap_weights(shift, offset):
    fraction = jnp.clip(-shift - offset.astype(jnp.float32), -0.5, 1.5)
    first, second, third, fourth = cubic_weights(fraction)
    nothing = jnp.zeros_like(fraction)
    at_arrival = offset == 0
    return (jnp.where(at_arrival, nothing, first), jnp.where(at_arrival, first, second),
            jnp.where(at_arrival, second, third), jnp.where(at_arrival, third, fourth),
            jnp.where(at_arrival, fourth, nothing))


def rolled_copies(padded):
    return [jnp.roll(padded, 2 - lon_step, axis=3) for lon_step in range(5)]


def interpolate(copies, field_ids, level_taps, row_taps, lon_taps):
    level_count = level_taps[0].shape[0]
    row_count = level_taps[0].shape[1]
    totals = [jnp.zeros(level_taps[0].shape, jnp.float32) for field_id in field_ids]
    for level_step in range(5):
        for row_step in range(5):
            outer = level_taps[level_step] * row_taps[row_step]
            for position in range(len(field_ids)):
                inner = jnp.zeros(outer.shape, jnp.float32)
                for lon_step in range(5):
                    block = copies[lon_step][level_step:level_step + level_count, field_ids[position],
                                             row_step:row_step + row_count, :]
                    inner = inner + lon_taps[lon_step] * block.astype(jnp.float32)
                totals[position] = totals[position] + outer * inner
    return totals


def departure(fields, wind_copies, tracer_copies, wind_ids, tracer_ids, eta_shift,
              row_offset, lon_offset, level_offset):
    east = fields[:, 0].astype(jnp.float32)
    north = fields[:, 1].astype(jnp.float32)
    level_taps = tap_weights(eta_shift.astype(jnp.float32), level_offset)
    shift_row = COURANT * north
    shift_lon = COURANT * east
    for sweep in range(ITERS):
        row_taps = tap_weights(shift_row, row_offset)
        lon_taps = tap_weights(shift_lon, lon_offset)
        east_found, north_found = interpolate(wind_copies, wind_ids, level_taps, row_taps, lon_taps)
        shift_row = 0.5 * COURANT * (north + north_found)
        shift_lon = 0.5 * COURANT * (east + east_found)
    row_taps = tap_weights(shift_row, row_offset)
    lon_taps = tap_weights(shift_lon, lon_offset)
    heat, moisture = interpolate(tracer_copies, tracer_ids, level_taps, row_taps, lon_taps)
    return jnp.stack([heat, moisture]).astype(jnp.bfloat16), jnp.stack([shift_row, shift_lon])


def split_halves(spectra, pairing):
    width = spectra.shape[-1]
    columns = lax.broadcasted_iota(jnp.int32, (pairing.shape[0], width), 1)
    first_part = columns < (width - 1 - pairing)[:, None]
    nothing = jnp.zeros((), spectra.dtype)
    return jnp.stack([jnp.where(first_part, spectra, nothing), jnp.where(first_part, nothing, spectra)])


def synthesis(pair_ids, lon_ids, lon_total):
    orders = jnp.stack([pair_ids, M - 1 - pair_ids])
    phase = ((orders[:, :, None] * lon_ids[None, None, :]) % lon_total).astype(jnp.float32) * (2.0 * math.pi / lon_total)
    weight = jnp.where(orders == 0, 1.0, 2.0).astype(jnp.float32)[:, :, None]
    return jnp.stack([weight * jnp.cos(phase), -weight * jnp.sin(phase)]).astype(jnp.bfloat16)


def reference(spectra, legendre, pairing, eta_shift, cells):
    table = jnp.transpose(legendre, (1, 0, 2, 3)).reshape(LAT, PAIRS, M + 1)
    halves = split_halves(spectra, pairing)
    coefficients = halves.reshape(16 * LEV, PAIRS, M + 1)

    def one_pair(pair_slot):
        rows_here = lax.dynamic_index_in_dim(table, pair_slot, 1, keepdims=False)
        columns_here = lax.dynamic_index_in_dim(coefficients, pair_slot, 1, keepdims=False)
        return jnp.dot(rows_here, columns_here.T, preferred_element_type=jnp.float32).astype(jnp.bfloat16)

    sums = lax.map(one_pair, jnp.arange(PAIRS, dtype=jnp.int32))
    sums = sums.reshape(PAIRS, LAT, 2, 2, 4 * LEV)
    basis = synthesis(pairing, jnp.arange(NLON, dtype=jnp.int32), NLON)
    grid = jnp.einsum('plhcf,chpj->flj', sums.astype(jnp.float32), basis.astype(jnp.float32)).astype(jnp.bfloat16)
    fields = grid.reshape(LEV, 4, LAT, NLON)
    padded = jnp.pad(fields, ((2, 2), (0, 0), (2, 2), (0, 0)))
    copies = rolled_copies(padded)
    grid_shape = (LEV, LAT, NLON)
    level_ids = lax.broadcasted_iota(jnp.int32, grid_shape, 0)
    row_ids = lax.broadcasted_iota(jnp.int32, grid_shape, 1)
    lon_ids = lax.broadcasted_iota(jnp.int32, grid_shape, 2)
    row_offset = cells[0] - row_ids
    lon_offset = (cells[1] - lon_ids + 2) % NLON - 2
    level_offset = cells[2] - level_ids
    return departure(fields, copies, copies, (0, 1), (2, 3), eta_shift, row_offset, lon_offset, level_offset)
```

```python
import functools
import math

import jax
import jax.numpy as jnp
import numpy as np
from jax import lax
from jax.experimental import pallas as pl
from jax.experimental.pallas import tpu as pltpu
from jax.sharding import PartitionSpec as P

ITERS = 2
COURANT = 0.8
MESH = pl.DeviceIdType.MESH
BF16 = jnp.bfloat16
F32 = jnp.float32
TAP = jnp.bfloat16
VMEM_LIMIT = 60 * 1024 * 1024


def nt_dot(a, b):
    return lax.dot_general(a, b, (((1,), (1,)), ((), ())), preferred_element_type=F32)


def tn_dot(a, b):
    return lax.dot_general(a, b, (((0,), (0,)), ((), ())), preferred_element_type=F32)


def comm_kernel(
    nb,
    nx,
    pairs,
    width,
    spec_ref,
    leg_ref,
    pair_ref,
    out_ref,
    specg,
    legs,
    sums_out,
    sums_in,
    stage,
    send,
    recv,
    halo,
    local_sem,
    spec_send,
    spec_recv,
    leg_send,
    leg_recv,
    x_send,
    x_recv,
    band_send,
    band_recv,
    halo_send,
    halo_recv,
):
    b = lax.axis_index("band")
    lev = lax.axis_index("lev")
    nlev = 2 * nx
    x = lev // 2
    core = lev % 2

    load = pltpu.make_async_copy(leg_ref, legs.at[core], local_sem)
    load.start()
    barrier = pltpu.get_barrier_semaphore()

    def greet_band(d, carry):
        pl.semaphore_signal(
            barrier, inc=1, device_id=(lax.rem(b + d, nb), lev), device_id_type=MESH
        )
        return carry

    for d in range(1, nlev):
        pl.semaphore_signal(
            barrier, inc=1, device_id=(b, lax.rem(lev + d, nlev)), device_id_type=MESH
        )
    lax.fori_loop(1, nb, greet_band, 0)
    for p in range(pairs):
        specg[x, p] = jnp.concatenate([spec_ref[0, p], spec_ref[1, p]], axis=0)
    load.wait()
    pl.semaphore_wait(barrier, nb - 1 + nlev - 1)

    spec_copies = []
    for d in range(1, nx):
        copy = pltpu.make_async_remote_copy(
            src_ref=specg.at[x],
            dst_ref=specg.at[x],
            send_sem=spec_send.at[d - 1],
            recv_sem=spec_recv.at[d - 1],
            device_id=(b, 2 * lax.rem(x + d, nx) + core),
            device_id_type=MESH,
        )
        copy.start()
        spec_copies.append(copy)
    leg_copy = pltpu.make_async_remote_copy(
        src_ref=legs.at[core],
        dst_ref=legs.at[core],
        send_sem=leg_send,
        recv_sem=leg_recv,
        device_id=(b, 2 * x + 1 - core),
        device_id_type=MESH,
    )
    leg_copy.start()
    leg_copy.wait()
    for copy in spec_copies:
        copy.wait()

    columns = lax.broadcasted_iota(jnp.int32, (16, width), 1)
    nothing = jnp.zeros((16, width), F32)
    for p in range(pairs):
        first_part = columns < (width - 1 - pair_ref[p])
        parts = []
        for other in range(nx):
            values = specg[other, p].astype(F32)
            parts.append(jnp.where(first_part, values, nothing))
            parts.append(jnp.where(first_part, nothing, values))
        rows = jnp.concatenate(parts, axis=0).astype(BF16)
        table = jnp.concatenate([legs[0, p], legs[1, p]], axis=0)
        total = nt_dot(rows, table).astype(BF16)
        for other in range(nx):
            sums_out[other, p] = total[other * 32 : (other + 1) * 32]
    sums_in[x] = sums_out[x]
    x_copies = []
    for d in range(1, nx):
        partner = lax.rem(x + d, nx)
        copy = pltpu.make_async_remote_copy(
            src_ref=sums_out.at[partner],
            dst_ref=sums_in.at[x],
            send_sem=x_send.at[d - 1],
            recv_sem=x_recv.at[d - 1],
            device_id=(b, 2 * partner + core),
            device_id_type=MESH,
        )
        copy.start()
        x_copies.append(copy)

    lanes = nx * 32
    lane = lax.broadcasted_iota(jnp.int32, (nb, lanes), 1)
    band = lax.broadcasted_iota(jnp.int32, (nb, lanes), 0)
    numbers = jnp.zeros((nb, lanes), jnp.int32)
    for p in range(pairs):
        numbers = jnp.where(lane == 2 * p, pair_ref[p] // 128, numbers)
        numbers = jnp.where(lane == 2 * p + 1, pair_ref[p] % 128, numbers)
    stage[pl.ds(3 * pairs, nb, stride=16), :] = numbers.astype(F32)
    square = (2 * nb, 2 * nb)
    unit = jnp.where(
        lax.broadcasted_iota(jnp.int32, square, 0) == lax.broadcasted_iota(jnp.int32, square, 1),
        1.0,
        0.0,
    ).astype(BF16)
    before = (lane // 32) % 2 == 0
    outside = ((band == 0) & before) | ((band == nb - 1) & jnp.logical_not(before))
    for copy in x_copies:
        copy.wait()
    for p in range(pairs):
        block = jnp.concatenate([sums_in[other, p] for other in range(nx)], axis=0)
        turned = nt_dot(unit, block)
        low, high = turned[:nb], turned[nb:]
        stage[pl.ds(2 * p, nb, stride=16), :] = low
        stage[pl.ds(2 * p + 1, nb, stride=16), :] = high
        edge = jnp.where(lane < 64, pltpu.roll(low, 32, 1), pltpu.roll(high, 96, 1))
        edge = jnp.where(before, pltpu.roll(edge, 1, 0), pltpu.roll(edge, nb - 1, 0))
        edge = jnp.where(outside, 0.0, edge)
        stage[pl.ds(2 * pairs + p, nb, stride=16), :] = edge
    send[...] = stage[...].reshape(nb, 16, lanes).astype(BF16)
    recv[b] = send[b]

    def send_band(d, carry):
        target = lax.rem(b + d, nb)
        pltpu.make_async_remote_copy(
            src_ref=send.at[target],
            dst_ref=recv.at[b],
            send_sem=band_send,
            recv_sem=band_recv,
            device_id=(target, lev),
            device_id_type=MESH,
        ).start()
        return carry

    lax.fori_loop(1, nb, send_band, 0)
    every = pltpu.make_async_remote_copy(
        src_ref=send.at[pl.ds(0, nb - 1)],
        dst_ref=recv.at[pl.ds(0, nb - 1)],
        send_sem=band_send,
        recv_sem=band_recv,
        device_id=(lax.rem(b + 1, nb), lev),
        device_id_type=MESH,
    )
    every.wait_recv()

    above = pltpu.make_async_remote_copy(
        src_ref=recv,
        dst_ref=halo.at[0],
        send_sem=halo_send.at[0],
        recv_sem=halo_recv.at[0],
        device_id=(b, lax.rem(lev + 1, nlev)),
        device_id_type=MESH,
    )
    below = pltpu.make_async_remote_copy(
        src_ref=recv,
        dst_ref=halo.at[1],
        send_sem=halo_send.at[1],
        recv_sem=halo_recv.at[1],
        device_id=(b, lax.rem(lev + nlev - 1, nlev)),
        device_id_type=MESH,
    )

    @pl.when(lev < nlev - 1)
    def _():
        above.start()

    @pl.when(lev > 0)
    def _():
        below.start()

    out_ref[1] = recv[...]
    every.wait_send()

    @pl.when(lev > 0)
    def _():
        above.wait_recv()
        out_ref[0] = halo[0]

    @pl.when(lev == 0)
    def _():
        out_ref[0] = jnp.zeros(halo.shape[1:], BF16)

    @pl.when(lev < nlev - 1)
    def _():
        below.wait_recv()
        out_ref[2] = halo[1]
        above.wait_send()

    @pl.when(lev == nlev - 1)
    def _():
        out_ref[2] = jnp.zeros(halo.shape[1:], BF16)

    @pl.when(lev > 0)
    def _():
        below.wait_send()


def gather_sums(spectra, legendre, pairing, nb, nx):
    pairs, width = spectra.shape[2], spectra.shape[3]
    spec = jnp.transpose(spectra, (0, 2, 1, 3))
    table = jnp.transpose(legendre[0], (1, 0, 2))
    lanes = nx * 32
    dma = pltpu.SemaphoreType.DMA
    return pl.pallas_call(
        functools.partial(comm_kernel, nb, nx, pairs, width),
        out_shape=jax.ShapeDtypeStruct((3, nb, 16, lanes), BF16),
        in_specs=[
            pl.BlockSpec(memory_space=pltpu.VMEM),
            pl.BlockSpec(memory_space=pl.ANY),
            pl.BlockSpec(memory_space=pltpu.SMEM),
        ],
        out_specs=pl.BlockSpec(memory_space=pltpu.VMEM),
        scratch_shapes=[
            pltpu.VMEM((nx, pairs, 16, width), BF16),
            pltpu.VMEM((2, pairs, nb, width), BF16),
            pltpu.VMEM((nx, pairs, 32, 2 * nb), BF16),
            pltpu.VMEM((nx, pairs, 32, 2 * nb), BF16),
            pltpu.VMEM((nb * 16, lanes), F32),
            pltpu.VMEM((nb, 16, lanes), BF16),
            pltpu.VMEM((nb, 16, lanes), BF16),
            pltpu.VMEM((2, nb, 16, lanes), BF16),
            dma,
            dma((nx - 1,)),
            dma((nx - 1,)),
            dma,
            dma,
            dma((nx - 1,)),
            dma((nx - 1,)),
            dma,
            dma,
            dma((2,)),
            dma((2,)),
        ],
        compiler_params=pltpu.CompilerParams(
            collective_id=0, has_side_effects=True, vmem_limit_bytes=VMEM_LIMIT
        ),
        name="sums",
    )(spec, table, pairing)


def lagrange_taps(shift, back):
    here = back == 0.0
    x = jnp.clip(back - shift, -0.5, 1.5)
    xm1, xm2, xp1 = x - 1.0, x - 2.0, x + 1.0
    tail = xm1 * xm2
    head = xp1 * x
    first = x * tail * (-1.0 / 6.0)
    second = xp1 * tail * 0.5
    third = head * xm2 * -0.5
    fourth = head * xm1 * (1.0 / 6.0)
    return (
        jnp.where(here, 0.0, first),
        jnp.where(here, first, second),
        jnp.where(here, second, third),
        jnp.where(here, third, fourth),
        jnp.where(here, fourth, 0.0),
    )


def weighted(taps, values):
    total = taps[0] * values[0]
    for tap, value in zip(taps[1:], values[1:]):
        total = total + tap * value
    return total


def fields_kernel(
    nb,
    nq,
    pairs,
    sums_ref,
    basis_ref,
    eta_ref,
    cells_ref,
    adv_ref,
    disp_ref,
    wide,
    slots,
    place,
    orders,
    coef,
    grid,
    near,
    points,
    eta_wide,
    found,
    adv_wide,
):
    qp = grid.shape[0] // 8 * 8 // 288
    npairs = nb * pairs
    kpad = place.shape[1]
    units = qp // 8
    rows = 8
    row0 = lax.axis_index("band") * rows
    lev0 = lax.axis_index("lev") * 2

    for g in range(3):
        wide[...] = sums_ref[g].astype(F32).reshape(nb * 16, 128)
        for p in range(pairs):
            for t, at in enumerate((2 * p, 2 * p + 1, 2 * pairs + p)):
                slots[p * nb : (p + 1) * nb, (g * 3 + t) * 128 : (g * 3 + t + 1) * 128] = wide[
                    pl.ds(at, nb, stride=16), :
                ].astype(BF16)
        if g == 1:
            numbers = wide[pl.ds(3 * pairs, nb, stride=16), :]
            order = lax.broadcasted_iota(jnp.int32, (nb, kpad), 1).astype(F32)
            for p in range(pairs):
                number = numbers[:, 2 * p : 2 * p + 1] * 128.0 + numbers[:, 2 * p + 1 : 2 * p + 2]
                place[p * nb : (p + 1) * nb, :] = jnp.where(order == number, 1.0, 0.0).astype(BF16)
    orders[...] = tn_dot(slots[...], place[...]).reshape(144, 8, kpad)
    for part in range(4):
        coef[:, part * kpad : (part + 1) * kpad] = jnp.concatenate(
            [orders[4 * m + part] for m in range(36)], axis=0
        ).astype(BF16)

    def synthesise(n, carry):
        values = jnp.dot(coef[...], basis_ref[n], preferred_element_type=F32).astype(BF16).astype(F32)
        width = values.shape[1] // 128
        for m in range(36):
            g, t, xs = m // 12, (m // 4) % 3, m % 4
            row = 2 + 2 * xs + t if t < 2 else (xs // 2 + (xs % 2) * 10)
            base = (row * 3 + g) * 8 * qp + 1
            for w in range(width):
                grid[pl.ds(base + n * width + w, 8, stride=qp), :] = values[
                    m * 8 : (m + 1) * 8, w * 128 : (w + 1) * 128
                ]
        return carry

    lax.fori_loop(0, basis_ref.shape[0], synthesise, 0)
    grid[pl.ds(0, 288, stride=qp), :] = grid[pl.ds(nq, 288, stride=qp), :]
    grid[pl.ds(nq + 1, 288, stride=qp), :] = grid[pl.ds(1, 288, stride=qp), :]

    lane = lax.broadcasted_iota(jnp.int32, (qp, 128), 1)

    def shift_rows(n, carry):
        row, field = n // 4, n % 4
        for step in range(5):
            c = step - 2
            moved = []
            for level in range(6):
                base = ((row * 6 + level) * 4 + field) * qp
                here = grid[pl.ds(base + 1, qp), :]
                if c > 0:
                    after = grid[pl.ds(base + 2, qp), :]
                    here = pltpu.roll(jnp.where(lane >= c, here, after), 128 - c, 1)
                elif c < 0:
                    ahead = grid[pl.ds(base, qp), :]
                    here = pltpu.roll(jnp.where(lane < 128 + c, here, ahead), -c, 1)
                moved.append(here)
            for a in range(5):
                pair = jnp.concatenate([moved[a], moved[a + 1]], axis=0).astype(TAP)
                for u in range(units):
                    near[row, u, field, step, a] = pair[u * 16 : (u + 1) * 16]
        return carry

    lax.fori_loop(0, 48, shift_rows, 0)

    for k in range(2):
        eta_wide[...] = eta_ref[k].astype(F32).reshape(nq * 8, 128)
        lon = (
            lax.broadcasted_iota(jnp.int32, (nq, 128), 0) * 128
            + lax.broadcasted_iota(jnp.int32, (nq, 128), 1)
        )
        for i in range(rows):
            part = pl.ds(i, nq, stride=8)
            at = pl.ds(k * qp, nq)
            points[i, 0, at, :] = jnp.where(cells_ref[0, k, part, :] == row0 + i, 0.0, 1.0)
            points[i, 1, at, :] = jnp.where(cells_ref[1, k, part, :] == lon, 0.0, 1.0)
            points[i, 2, at, :] = jnp.where(cells_ref[2, k, part, :] == lev0 + k, 0.0, 1.0)
            points[i, 3, at, :] = eta_wide[part, :]

    def depart(n, carry):
        i, u = n // units, n % units
        at = pl.ds(pl.multiple_of(u * 16, 16), 16)
        row_back, lon_back = points[i, 0, at, :], points[i, 1, at, :]
        level_taps = [
            tap.astype(TAP) for tap in lagrange_taps(points[i, 3, at, :], points[i, 2, at, :])
        ]

        def level_sums(field):
            return [
                [
                    weighted(level_taps, [near[i + b, u, field, c, a] for a in range(5)])
                    for c in range(5)
                ]
                for b in range(5)
            ]

        def horizontal(sums, row_taps, lon_taps):
            return weighted(row_taps, [weighted(lon_taps, sums[b]).astype(F32) for b in range(5)])

        east = near[i + 2, u, 0, 2, 2].astype(F32)
        north = near[i + 2, u, 1, 2, 2].astype(F32)
        east_sums, north_sums = level_sums(0), level_sums(1)
        shift_row, shift_lon = COURANT * north, COURANT * east
        for sweep in range(ITERS):
            row_taps = lagrange_taps(shift_row, row_back)
            lon_taps = [tap.astype(TAP) for tap in lagrange_taps(shift_lon, lon_back)]
            shift_row = 0.5 * COURANT * (north + horizontal(north_sums, row_taps, lon_taps))
            shift_lon = 0.5 * COURANT * (east + horizontal(east_sums, row_taps, lon_taps))
        found[i, 0, at, :] = shift_row
        found[i, 1, at, :] = shift_lon
        row_taps = lagrange_taps(shift_row, row_back)
        lon_taps = [tap.astype(TAP) for tap in lagrange_taps(shift_lon, lon_back)]
        found[i, 2, at, :] = horizontal(level_sums(2), row_taps, lon_taps)
        found[i, 3, at, :] = horizontal(level_sums(3), row_taps, lon_taps)
        return carry

    lax.fori_loop(0, rows * units, depart, 0)
    for k in range(2):
        for i in range(rows):
            part = pl.ds(i, nq, stride=8)
            at = pl.ds(k * qp, nq)
            for which in range(2):
                disp_ref[which, k, part, :] = found[i, which, at, :]
                adv_wide[which, k, part, :] = found[i, 2 + which, at, :]
    adv_ref[...] = adv_wide[...].reshape(adv_ref.shape).astype(BF16)


def basis_table(total, lon_total, block):
    npairs = total // 2
    kpad = -(-npairs // 128) * 128
    r = np.arange(npairs, dtype=np.int64)
    j = np.arange(lon_total, dtype=np.int64)
    table = np.zeros((2, 2, kpad, lon_total), np.float32)
    for half, order in enumerate((r, total - 1 - r)):
        angle = (2.0 * math.pi / lon_total) * ((order[:, None] * j[None, :]) % lon_total)
        weight = np.where(order == 0, 1.0, 2.0)[:, None]
        table[half, 0, :npairs] = weight * np.cos(angle)
        table[half, 1, :npairs] = -weight * np.sin(angle)
    table = table.reshape(4 * kpad, lon_total // block, block).transpose(1, 0, 2)
    return jnp.asarray(table.astype(BF16)), kpad


def depart_fields(sums, eta_shift, cells, nb, pairs, total):
    lon_total = eta_shift.shape[2]
    nq = lon_total // 128
    qp = -(-(nq + 2) // 8) * 8
    basis, kpad = basis_table(total, lon_total, 256)
    tiles = lambda a: jnp.swapaxes(a.reshape(a.shape[:-1] + (nq, 128)), -3, -2)
    eta = tiles(eta_shift)
    cells = tiles(cells).reshape(3, 2, nq * 8, 128)
    vmem = pl.BlockSpec(memory_space=pltpu.VMEM)
    adv, disp = pl.pallas_call(
        functools.partial(fields_kernel, nb, nq, pairs),
        out_shape=(
            jax.ShapeDtypeStruct((2, 2, nq, 8, 128), BF16),
            jax.ShapeDtypeStruct((2, 2, nq * 8, 128), F32),
        ),
        in_specs=[vmem] * 4,
        out_specs=(vmem, vmem),
        scratch_shapes=[
            pltpu.VMEM((nb * 16, 128), F32),
            pltpu.VMEM((nb * pairs, 9 * 128), BF16),
            pltpu.VMEM((nb * pairs, kpad), BF16),
            pltpu.VMEM((144, 8, kpad), F32),
            pltpu.VMEM((288, 4 * kpad), BF16),
            pltpu.VMEM((288 * qp + 8, 128), F32),
            pltpu.VMEM((12, qp // 8, 4, 5, 5, 16, 128), TAP),
            pltpu.VMEM((8, 4, 2 * qp, 128), F32),
            pltpu.VMEM((nq * 8, 128), F32),
            pltpu.VMEM((8, 4, 2 * qp, 128), F32),
            pltpu.VMEM((2, 2, nq * 8, 128), F32),
        ],
        compiler_params=pltpu.CompilerParams(vmem_limit_bytes=VMEM_LIMIT),
        name="fields",
    )(sums, basis, eta, cells)
    whole = lambda a: jnp.swapaxes(a, -3, -2).reshape(2, 2, 8, lon_total)
    return whole(adv), whole(disp.reshape(2, 2, nq, 8, 128))


def per_device(spectra, legendre, pairing, eta_shift, cells):
    nb = legendre.shape[1]
    pairs, width = spectra.shape[2], spectra.shape[3]
    nx = lax.axis_size("lev") // 2
    sums = gather_sums(spectra, legendre, pairing, nb, nx)
    return depart_fields(sums, eta_shift, cells, nb, pairs, width - 1)


def solution(mesh):
    return jax.shard_map(
        per_device,
        mesh=mesh,
        in_specs=(
            P(None, "lev", "band", None),
            P("lev", None, "band", None),
            P("band"),
            P("lev", "band", None),
            P(None, "lev", "band", None),
        ),
        out_specs=(P(None, "lev", "band", None), P(None, "lev", "band", None)),
        check_vma=False,
    )
```

```python
import functools
import math

import jax
import jax.numpy as jnp
import numpy as np
from jax import lax
from jax.experimental import pallas as pl
from jax.experimental.pallas import tpu as pltpu
from jax.sharding import PartitionSpec as P

ITERS = 2
COURANT = 0.8
MESH = pl.DeviceIdType.MESH
BF16 = jnp.bfloat16
F32 = jnp.float32
TAP = jnp.bfloat16
VMEM_LIMIT = 60 * 1024 * 1024
GROUPS = 8


def nt_dot(a, b):
    return lax.dot_general(a, b, (((1,), (1,)), ((), ())), preferred_element_type=F32)


def tn_dot(a, b):
    return lax.dot_general(a, b, (((0,), (0,)), ((), ())), preferred_element_type=F32)


def comm_kernel(
    nb,
    nx,
    pairs,
    width,
    spec_ref,
    leg_ref,
    pair_ref,
    out_ref,
    raw,
    specg,
    last,
    legs,
    sums_out,
    sums_in,
    stage,
    send,
    recv,
    nothing,
    load_sem,
    last_send,
    last_recv,
    spec_send,
    spec_recv,
    leg_send,
    leg_recv,
    x_send,
    x_recv,
    band_send,
    band_recv,
    halo_send,
    halo_recv,
    own_sem,
    lev_ready,
    band_ready,
):
    b = lax.axis_index("band")
    lev = lax.axis_index("lev")
    nlev = 2 * nx
    x = lev // 2
    core = lev % 2
    group = max(1, nb // GROUPS)

    def remote(src, dst, send_sem, recv_sem, band, level):
        return pltpu.make_async_remote_copy(
            src_ref=src,
            dst_ref=dst,
            send_sem=send_sem,
            recv_sem=recv_sem,
            device_id=(band, level),
            device_id_type=MESH,
        )

    def signal(semaphore, band, level):
        pl.semaphore_signal(semaphore, inc=1, device_id=(band, level), device_id_type=MESH)

    side = math.isqrt(nb)

    def hops(d):
        return sum(min(n, side - n) for n in (d // side, d % side))

    order = sorted(range(1, nb), key=lambda d: -hops(d))
    sibling = (b, 2 * x + 1 - core)

    loads = (
        pltpu.make_async_copy(spec_ref, raw, load_sem.at[0]),
        pltpu.make_async_copy(leg_ref, legs.at[:, core], load_sem.at[1]),
    )
    for load in loads:
        load.start()
    barrier = pltpu.get_barrier_semaphore()

    for d in range(1, nx):
        signal(barrier, b, 2 * lax.rem(x + d, nx))

    @pl.when(core == 1)
    def _():
        signal(barrier, b, 2 * x)

    loads[0].wait()
    tail = jnp.zeros((16, 128), F32)
    place = lax.broadcasted_iota(jnp.int32, (16, 128), 1)
    for p in range(pairs):
        own = jnp.concatenate([raw[0, p], raw[1, p]], axis=0)
        specg[p, 0] = own[:, : width - 1]
        tail = jnp.where(place == p, own[:, width - 1 :].astype(F32), tail)
    last[0] = tail.astype(BF16)

    @pl.when(core == 0)
    def _():
        pl.semaphore_wait(barrier, nlev - 1)
        signal(lev_ready, *sibling)

    @pl.when(core == 1)
    def _():
        pl.semaphore_wait(lev_ready, 1)

    for p in range(pairs):
        for d in sorted(range(1, nx), key=lambda d: -min(d, nx - d)):
            target = 2 * lax.rem(x + d, nx) + core
            if p == 0:
                remote(last.at[0], last.at[d], last_send, last_recv, b, target).start()
            remote(specg.at[p, 0], specg.at[p, d], spec_send, spec_recv.at[p], b, target).start()
        if p == 0:
            loads[1].wait()
        remote(legs.at[p, core], legs.at[p, core], leg_send, leg_recv.at[p], *sibling).start()

    for d in order:
        signal(barrier, lax.rem(b + d, nb), 2 * x + 1)
    nothing[...] = jnp.zeros(nothing.shape, BF16)

    columns = lax.broadcasted_iota(jnp.int32, (16, width - 1), 1)
    zero = jnp.zeros((16, width - 1), F32)
    no_tail = jnp.zeros((16, 1), F32)
    others = last.at[pl.ds(1, nx - 1)]
    remote(others, others, last_send, last_recv, *sibling).wait_recv()
    for p in range(pairs):
        others = specg.at[p, pl.ds(1, nx - 1)]
        remote(others, others, spec_send, spec_recv.at[p], *sibling).wait_recv()
        table_ref = legs.at[p, 0]
        remote(table_ref, table_ref, leg_send, leg_recv.at[p], *sibling).wait_recv()
        first_part = columns < (width - 1 - pair_ref[p])
        parts = []
        for d in range(nx):
            values = specg[p, d].astype(F32)
            tail = last[d].astype(F32)[:, p : p + 1]
            parts.append(jnp.concatenate([jnp.where(first_part, values, zero), no_tail], axis=1))
            parts.append(jnp.concatenate([jnp.where(first_part, zero, values), tail], axis=1))
        rows = jnp.concatenate(parts, axis=0).astype(BF16)
        table = jnp.concatenate([legs[p, 0], legs[p, 1]], axis=0)
        total = nt_dot(rows, table).astype(BF16)
        for d in range(nx):
            sums_out[p, d] = total[d * 32 : (d + 1) * 32]
        sums_in[p, x] = total[:32]
        for d in range(nx - 1, 0, -1):
            remote(
                sums_out.at[p, d],
                sums_in.at[p, x],
                x_send,
                x_recv.at[p],
                b,
                2 * lax.rem(x + nx - d, nx) + core,
            ).start()

    lanes = nx * 32
    lane = lax.broadcasted_iota(jnp.int32, (nb, lanes), 1)
    band = lax.broadcasted_iota(jnp.int32, (nb, lanes), 0)
    numbers = jnp.zeros((nb, lanes), jnp.int32)
    for p in range(pairs):
        numbers = jnp.where(lane == 2 * p, pair_ref[p] // 128, numbers)
        numbers = jnp.where(lane == 2 * p + 1, pair_ref[p] % 128, numbers)
    stage[pl.ds(3 * pairs, nb, stride=16), :] = numbers.astype(F32)
    square = (2 * nb, 2 * nb)
    unit = jnp.where(
        lax.broadcasted_iota(jnp.int32, square, 0) == lax.broadcasted_iota(jnp.int32, square, 1),
        1.0,
        0.0,
    ).astype(BF16)
    before = (lane // 32) % 2 == 0
    outside = ((band == 0) & before) | ((band == nb - 1) & jnp.logical_not(before))
    for p in range(pairs):
        others = sums_out.at[p, pl.ds(1, nx - 1)]
        remote(others, others, x_send, x_recv.at[p], *sibling).wait_recv()
        block = jnp.concatenate([sums_in[p, other] for other in range(nx)], axis=0)
        turned = nt_dot(unit, block)
        low, high = turned[:nb], turned[nb:]
        stage[pl.ds(2 * p, nb, stride=16), :] = low
        stage[pl.ds(2 * p + 1, nb, stride=16), :] = high
        edge = jnp.where(lane < 64, pltpu.roll(low, 32, 1), pltpu.roll(high, 96, 1))
        edge = jnp.where(before, pltpu.roll(edge, 1, 0), pltpu.roll(edge, nb - 1, 0))
        edge = jnp.where(outside, 0.0, edge)
        stage[pl.ds(2 * pairs + p, nb, stride=16), :] = edge
    send[...] = stage[...].reshape(nb, 16, lanes).astype(BF16)
    recv[nb - 1] = send[b]

    @pl.when(core == 1)
    def _():
        pl.semaphore_wait(barrier, 2 * (nb - 1))
        signal(band_ready, *sibling)

    @pl.when(core == 0)
    def _():
        pl.semaphore_wait(band_ready, 1)

    for n, d in enumerate(order):
        target = lax.rem(b + d, nb)
        remote(
            send.at[target], recv.at[n], band_send, band_recv.at[n // group], target, lev
        ).start()

    above = (b, lax.rem(lev + 1, nlev))
    below = (b, lax.rem(lev + nlev - 1, nlev))
    lowest = lev == 0
    highest = lev == nlev - 1

    @pl.when(lowest)
    def _():
        pltpu.make_async_copy(nothing, out_ref.at[0], own_sem.at[0]).start()

    @pl.when(highest)
    def _():
        pltpu.make_async_copy(nothing, out_ref.at[2], own_sem.at[0]).start()

    for g in reversed(range(GROUPS)):
        end = min(nb - 1, (g + 1) * group)
        if end > g * group:
            arrived = recv.at[pl.ds(g * group, end - g * group)]
            remote(arrived, arrived, band_send, band_recv.at[g], *sibling).wait_recv()
        part = pl.ds(g * group, group)

        @pl.when(lev < nlev - 1)
        def _():
            remote(
                recv.at[part], out_ref.at[0, part], halo_send.at[0], halo_recv.at[0], *above
            ).start()

        @pl.when(lev > 0)
        def _():
            remote(
                recv.at[part], out_ref.at[2, part], halo_send.at[1], halo_recv.at[1], *below
            ).start()

    own = pltpu.make_async_copy(recv, out_ref.at[1], own_sem.at[1])
    own.start()

    others = last.at[pl.ds(1, nx - 1)]
    remote(others, others, last_send, last_recv, *sibling).wait_send()
    others = specg.at[:, pl.ds(1, nx - 1)]
    remote(others, others, spec_send, spec_recv.at[0], *sibling).wait_send()
    tables = legs.at[:, 0]
    remote(tables, tables, leg_send, leg_recv.at[0], *sibling).wait_send()
    others = sums_out.at[:, pl.ds(1, nx - 1)]
    remote(others, others, x_send, x_recv.at[0], *sibling).wait_send()
    arrived = recv.at[pl.ds(0, nb - 1)]
    remote(arrived, arrived, band_send, band_recv.at[0], *sibling).wait_send()
    own.wait()

    up = remote(recv, out_ref.at[0], halo_send.at[0], halo_recv.at[0], *above)
    down = remote(recv, out_ref.at[2], halo_send.at[1], halo_recv.at[1], *below)

    @pl.when(lev > 0)
    def _():
        up.wait_recv()
        down.wait_send()

    @pl.when(lev < nlev - 1)
    def _():
        down.wait_recv()
        up.wait_send()

    @pl.when(lowest)
    def _():
        pltpu.make_async_copy(nothing, out_ref.at[0], own_sem.at[0]).wait()

    @pl.when(highest)
    def _():
        pltpu.make_async_copy(nothing, out_ref.at[2], own_sem.at[0]).wait()


def gather_sums(spectra, legendre, pairing, nb, nx):
    pairs, width = spectra.shape[2], spectra.shape[3]
    spec = jnp.transpose(spectra, (0, 2, 1, 3))
    table = jnp.transpose(legendre[0], (1, 0, 2))
    lanes = nx * 32
    dma = pltpu.SemaphoreType.DMA
    anywhere = pl.BlockSpec(memory_space=pl.ANY)
    return pl.pallas_call(
        functools.partial(comm_kernel, nb, nx, pairs, width),
        out_shape=jax.ShapeDtypeStruct((3, nb, 16, lanes), BF16),
        in_specs=[anywhere, anywhere, pl.BlockSpec(memory_space=pltpu.SMEM)],
        out_specs=anywhere,
        scratch_shapes=[
            pltpu.VMEM(spec.shape, BF16),
            pltpu.VMEM((pairs, nx, 16, width - 1), BF16),
            pltpu.VMEM((nx, 16, 128), BF16),
            pltpu.VMEM((pairs, 2, nb, width), BF16),
            pltpu.VMEM((pairs, nx, 32, 2 * nb), BF16),
            pltpu.VMEM((pairs, nx, 32, 2 * nb), BF16),
            pltpu.VMEM((nb * 16, lanes), F32),
            pltpu.VMEM((nb, 16, lanes), BF16),
            pltpu.VMEM((nb, 16, lanes), BF16),
            pltpu.VMEM((nb, 16, lanes), BF16),
            dma((2,)),
            dma,
            dma,
            dma,
            dma((pairs,)),
            dma,
            dma((pairs,)),
            dma,
            dma((pairs,)),
            dma,
            dma((GROUPS,)),
            dma((2,)),
            dma((2,)),
            dma((2,)),
            pltpu.SemaphoreType.REGULAR,
            pltpu.SemaphoreType.REGULAR,
        ],
        compiler_params=pltpu.CompilerParams(
            collective_id=0, has_side_effects=True, vmem_limit_bytes=VMEM_LIMIT
        ),
        name="sums",
    )(spec, table, pairing)


def lagrange_taps(shift, back):
    here = back == 0.0
    x = jnp.clip(back - shift, -0.5, 1.5)
    xm1, xm2, xp1 = x - 1.0, x - 2.0, x + 1.0
    tail = xm1 * xm2
    head = xp1 * x
    first = x * tail * (-1.0 / 6.0)
    second = xp1 * tail * 0.5
    third = head * xm2 * -0.5
    fourth = head * xm1 * (1.0 / 6.0)
    return (
        jnp.where(here, 0.0, first),
        jnp.where(here, first, second),
        jnp.where(here, second, third),
        jnp.where(here, third, fourth),
        jnp.where(here, fourth, 0.0),
    )


def weighted(taps, values):
    total = taps[0] * values[0]
    for tap, value in zip(taps[1:], values[1:]):
        total = total + tap * value
    return total


def fields_kernel(
    nb,
    nq,
    pairs,
    sums_hbm,
    basis_ref,
    eta_ref,
    cells_ref,
    adv_ref,
    disp_ref,
    wide,
    slots,
    place,
    orders,
    coef,
    basis,
    grid,
    near,
    eta,
    cells,
    points,
    eta_wide,
    found,
    adv_wide,
    sums_ref,
    basis_sem,
    point_sem,
    sums_sem,
):
    qp = grid.shape[0] // 8 * 8 // 288
    half = nb * pairs // 2
    window = place.shape[1] // 2
    lon_half = nq * 64
    units = qp // 8
    rows = 8
    row0 = lax.axis_index("band") * rows
    lev0 = lax.axis_index("lev") * 2

    sums_copies = [
        pltpu.make_async_copy(sums_hbm.at[g], sums_ref.at[g], sums_sem.at[g]) for g in range(3)
    ]
    for copy in sums_copies:
        copy.start()
    blocks = [(start, min(256, lon_half - start)) for start in range(0, lon_half, 256)]
    basis_copies = []
    for n, (start, size) in enumerate(blocks):
        part = pl.ds(start, size)
        copy = pltpu.make_async_copy(
            basis_ref.at[:, :, part], basis.at[:, :, part], basis_sem.at[n]
        )
        copy.start()
        basis_copies.append(copy)
    point_copies = (
        pltpu.make_async_copy(eta_ref, eta, point_sem.at[0]),
        pltpu.make_async_copy(cells_ref, cells, point_sem.at[1]),
    )
    for copy in point_copies:
        copy.start()

    for g in range(3):
        sums_copies[g].wait()
        wide[...] = sums_ref[g].astype(F32).reshape(nb * 16, 128)
        for p in range(pairs):
            for t, at in enumerate((2 * p, 2 * p + 1, 2 * pairs + p)):
                slots[p * nb : (p + 1) * nb, (g * 3 + t) * 128 : (g * 3 + t + 1) * 128] = wide[
                    pl.ds(at, nb, stride=16), :
                ].astype(BF16)
        if g == 1:
            numbers = wide[pl.ds(3 * pairs, nb, stride=16), :].astype(jnp.int32)
            column = lax.broadcasted_iota(jnp.int32, (nb, 2 * window), 1)
            order = jnp.where(column < window, 2 * column, 2 * (column - window) + 1)
            for p in range(pairs):
                number = numbers[:, 2 * p : 2 * p + 1] * 128 + numbers[:, 2 * p + 1 : 2 * p + 2]
                place[p * nb : (p + 1) * nb, :] = jnp.where(order == number, 1.0, 0.0).astype(BF16)
    orders[...] = tn_dot(slots[...], place[...]).reshape(144, 8, 2 * window)
    for parity in range(2):
        for part in range(4):
            first = window * ((part // 2 + parity) % 2)
            coef[parity, part] = jnp.concatenate(
                [orders[4 * m + part, :, first : first + window] for m in range(36)], axis=0
            ).astype(BF16)

    for (start, size), copy in zip(blocks, basis_copies):
        copy.wait()
        even, odd = [
            sum(
                jnp.dot(
                    coef[parity, part, :, :half],
                    basis[parity, part * half : (part + 1) * half, start : start + size],
                    preferred_element_type=F32,
                )
                for part in range(4)
            )
            for parity in range(2)
        ]
        for turn, values in enumerate((even + odd, even - odd)):
            for m in range(36):
                g, t, xs = m // 12, (m // 4) % 3, m % 4
                row = 2 + 2 * xs + t if t < 2 else (xs // 2 + (xs % 2) * 10)
                base = (row * 3 + g) * 8 * qp + 1 + (start + turn * lon_half) // 128
                for w in range(size // 128):
                    grid[pl.ds(base + w, 8, stride=qp), :] = values[
                        m * 8 : (m + 1) * 8, w * 128 : (w + 1) * 128
                    ]
    grid[pl.ds(0, 288, stride=qp), :] = grid[pl.ds(nq, 288, stride=qp), :]
    grid[pl.ds(nq + 1, 288, stride=qp), :] = grid[pl.ds(1, 288, stride=qp), :]

    lane = lax.broadcasted_iota(jnp.int32, (16, 128), 1).astype(F32).astype(TAP)
    inside = {c: (lane >= c if c > 0 else lane < 128 + c) for c in (-2, -1, 1, 2)}

    def shift_fields(n, carry):
        row, level = n // 6, n % 6
        for two in range(2):
            for t in range(units):

                def block(offset):
                    return jnp.concatenate(
                        [
                            grid[pl.ds((n * 4 + field) * qp + 8 * t + offset, 8), :]
                            for field in (2 * two, 2 * two + 1)
                        ],
                        axis=0,
                    ).astype(TAP)

                ahead, here, after = block(0), block(1), block(2)
                for c in range(-2, 3):
                    value = here
                    if c > 0:
                        value = pltpu.roll(jnp.where(inside[c], here, after), 128 - c, 1)
                    elif c < 0:
                        value = pltpu.roll(jnp.where(inside[c], here, ahead), -c, 1)
                    near[row, level, t, two, c + 2] = value
        return carry

    lax.fori_loop(0, 72, shift_fields, 0, unroll=8)

    for copy in point_copies:
        copy.wait()
    for k in range(2):
        eta_wide[...] = eta[k].astype(F32).reshape(nq * 8, 128)
        lon = (
            lax.broadcasted_iota(jnp.int32, (nq, 128), 0) * 128
            + lax.broadcasted_iota(jnp.int32, (nq, 128), 1)
        )
        for i in range(rows):
            part = pl.ds(i, nq, stride=8)
            at = pl.ds(k * qp, nq)
            points[i, 0, at, :] = jnp.where(cells[0, k, part, :] == row0 + i, 0.0, 1.0)
            points[i, 1, at, :] = jnp.where(cells[1, k, part, :] == lon, 0.0, 1.0)
            points[i, 2, at, :] = jnp.where(cells[2, k, part, :] == lev0 + k, 0.0, 1.0)
            points[i, 3, at, :] = eta_wide[part, :]

    def double(taps):
        return [jnp.concatenate([tap, tap], axis=0).astype(TAP) for tap in taps]

    def depart(n, carry):
        i, k, t = n // (2 * units), (n // units) % 2, n % units
        at = pl.ds(pl.multiple_of((k * units + t) * 8, 8), 8)
        row_back, lon_back = points[i, 0, at, :], points[i, 1, at, :]
        level_taps = double(lagrange_taps(points[i, 3, at, :], points[i, 2, at, :]))

        def level_sums(two):
            return [
                [
                    weighted(level_taps, [near[i + b, k + a, t, two, c] for a in range(5)])
                    for c in range(5)
                ]
                for b in range(5)
            ]

        def horizontal(sums, shift_row, shift_lon):
            row_taps = lagrange_taps(shift_row, row_back)
            lon_taps = double(lagrange_taps(shift_lon, lon_back))
            lines = [weighted(lon_taps, sums[b]).astype(F32) for b in range(5)]
            return [
                weighted(row_taps, [line[s * 8 : (s + 1) * 8] for line in lines]) for s in range(2)
            ]

        wind = near[i + 2, k + 2, t, 0, 2].astype(F32)
        east, north = wind[:8], wind[8:]
        wind_sums = level_sums(0)
        shift_row, shift_lon = COURANT * north, COURANT * east
        for sweep in range(ITERS):
            east_found, north_found = horizontal(wind_sums, shift_row, shift_lon)
            shift_row = 0.5 * COURANT * (north + north_found)
            shift_lon = 0.5 * COURANT * (east + east_found)
        found[i, 0, at, :] = shift_row
        found[i, 1, at, :] = shift_lon
        heat, moisture = horizontal(level_sums(1), shift_row, shift_lon)
        found[i, 2, at, :] = heat
        found[i, 3, at, :] = moisture
        return carry

    lax.fori_loop(0, rows * 2 * units, depart, 0, unroll=4)
    for k in range(2):
        for i in range(rows):
            part = pl.ds(i, nq, stride=8)
            at = pl.ds(k * qp, nq)
            for which in range(2):
                disp_ref[which, k, part, :] = found[i, which, at, :]
                adv_wide[which, k, part, :] = found[i, 2 + which, at, :]
    adv_ref[...] = adv_wide[...].reshape(adv_ref.shape).astype(BF16)


def basis_table(total, lon_total):
    npairs = total // 2
    m = np.arange(npairs // 2, dtype=np.int64)
    j = np.arange(lon_total // 2, dtype=np.int64)
    orders = ((2 * m, total - 2 - 2 * m), (2 * m + 1, total - 1 - 2 * m))
    table = np.zeros((2, 2, 2, npairs // 2, lon_total // 2), np.float32)
    for parity in range(2):
        for half in range(2):
            order = orders[parity][half][:, None]
            angle = (2.0 * math.pi / lon_total) * ((order * j[None, :]) % lon_total)
            weight = np.where(order == 0, 1.0, 2.0)
            table[parity, half, 0] = weight * np.cos(angle)
            table[parity, half, 1] = -weight * np.sin(angle)
    return jnp.asarray(table.reshape(2, 2 * npairs, lon_total // 2).astype(BF16))


def depart_fields(sums, eta_shift, cells, nb, pairs, total):
    lon_total = eta_shift.shape[2]
    nq = lon_total // 128
    qp = -(-(nq + 2) // 8) * 8
    basis = basis_table(total, lon_total)
    window = -(-total // 4 // 128) * 128
    tiles = lambda a: jnp.swapaxes(a.reshape(a.shape[:-1] + (nq, 128)), -3, -2)
    eta = tiles(eta_shift)
    cells = tiles(cells).reshape(3, 2, nq * 8, 128)
    vmem = pl.BlockSpec(memory_space=pltpu.VMEM)
    anywhere = pl.BlockSpec(memory_space=pl.ANY)
    adv, disp = pl.pallas_call(
        functools.partial(fields_kernel, nb, nq, pairs),
        out_shape=(
            jax.ShapeDtypeStruct((2, 2, nq, 8, 128), BF16),
            jax.ShapeDtypeStruct((2, 2, nq * 8, 128), F32),
        ),
        in_specs=[anywhere] * 4,
        out_specs=(vmem, vmem),
        scratch_shapes=[
            pltpu.VMEM((nb * 16, 128), F32),
            pltpu.VMEM((nb * pairs, 9 * 128), BF16),
            pltpu.VMEM((nb * pairs, 2 * window), BF16),
            pltpu.VMEM((144, 8, 2 * window), F32),
            pltpu.VMEM((2, 4, 288, window), BF16),
            pltpu.VMEM(basis.shape, BF16),
            pltpu.VMEM((288 * qp + 8, 128), F32),
            pltpu.VMEM((12, 6, qp // 8, 2, 5, 16, 128), TAP),
            pltpu.VMEM(eta.shape, BF16),
            pltpu.VMEM(cells.shape, jnp.int32),
            pltpu.VMEM((8, 4, 2 * qp, 128), F32),
            pltpu.VMEM((nq * 8, 128), F32),
            pltpu.VMEM((8, 4, 2 * qp, 128), F32),
            pltpu.VMEM((2, 2, nq * 8, 128), F32),
            pltpu.VMEM(sums.shape, BF16),
            pltpu.SemaphoreType.DMA((-(-lon_total // 512),)),
            pltpu.SemaphoreType.DMA((2,)),
            pltpu.SemaphoreType.DMA((3,)),
        ],
        compiler_params=pltpu.CompilerParams(vmem_limit_bytes=VMEM_LIMIT),
        name="fields",
    )(sums, basis, eta, cells)
    whole = lambda a: jnp.swapaxes(a, -3, -2).reshape(2, 2, 8, lon_total)
    return whole(adv), whole(disp.reshape(2, 2, nq, 8, 128))


def per_device(spectra, legendre, pairing, eta_shift, cells):
    nb = legendre.shape[1]
    pairs, width = spectra.shape[2], spectra.shape[3]
    nx = lax.axis_size("lev") // 2
    sums = gather_sums(spectra, legendre, pairing, nb, nx)
    return depart_fields(sums, eta_shift, cells, nb, pairs, width - 1)


def solution(mesh):
    return jax.shard_map(
        per_device,
        mesh=mesh,
        in_specs=(
            P(None, "lev", "band", None),
            P("lev", None, "band", None),
            P("band"),
            P("lev", "band", None),
            P(None, "lev", "band", None),
        ),
        out_specs=(P(None, "lev", "band", None), P(None, "lev", "band", None)),
        check_vma=False,
    )
```

```python
import functools
import math

import jax
import jax.numpy as jnp
import numpy as np
from jax import lax
from jax.experimental import pallas as pl
from jax.experimental.pallas import tpu as pltpu
from jax.sharding import PartitionSpec as P

ITERS = 2
COURANT = 0.8
MESH = pl.DeviceIdType.MESH
BF16 = jnp.bfloat16
F32 = jnp.float32
TAP = jnp.bfloat16
VMEM_LIMIT = 60 * 1024 * 1024
GROUPS = 8


def nt_dot(a, b):
    return lax.dot_general(a, b, (((1,), (1,)), ((), ())), preferred_element_type=F32)


def tn_dot(a, b):
    return lax.dot_general(a, b, (((0,), (0,)), ((), ())), preferred_element_type=F32)


def gather_sums(
    nb,
    nx,
    pairs,
    width,
    after_sums,
    after_sends,
    after_own,
    spec_ref,
    leg_ref,
    pair_ref,
    recv,
    halo,
    raw,
    specg,
    last,
    legs,
    sums_out,
    sums_in,
    stage,
    send,
    load_sem,
    last_send,
    last_recv,
    spec_send,
    spec_recv,
    leg_send,
    leg_recv,
    x_send,
    x_recv,
    band_send,
    band_recv,
    halo_send,
    halo_recv,
    lev_ready,
    band_ready,
):
    b = lax.axis_index("band")
    lev = lax.axis_index("lev")
    nlev = 2 * nx
    x = lev // 2
    core = lev % 2
    group = max(1, nb // GROUPS)

    def remote(src, dst, send_sem, recv_sem, band, level):
        return pltpu.make_async_remote_copy(
            src_ref=src,
            dst_ref=dst,
            send_sem=send_sem,
            recv_sem=recv_sem,
            device_id=(band, level),
            device_id_type=MESH,
        )

    def signal(semaphore, band, level):
        pl.semaphore_signal(semaphore, inc=1, device_id=(band, level), device_id_type=MESH)

    side = math.isqrt(nb)

    def hops(d):
        return sum(min(n, side - n) for n in (d // side, d % side))

    order = sorted(range(1, nb), key=lambda d: -hops(d))
    sibling = (b, 2 * x + 1 - core)

    loads = (
        pltpu.make_async_copy(spec_ref, raw, load_sem.at[0]),
        pltpu.make_async_copy(leg_ref, legs.at[:, core], load_sem.at[1]),
    )
    for load in loads:
        load.start()
    barrier = pltpu.get_barrier_semaphore()

    for d in range(1, nx):
        signal(barrier, b, 2 * lax.rem(x + d, nx))

    @pl.when(core == 1)
    def _():
        signal(barrier, b, 2 * x)

    loads[0].wait()
    tail = jnp.zeros((16, 128), F32)
    place = lax.broadcasted_iota(jnp.int32, (16, 128), 1)
    for p in range(pairs):
        own = jnp.concatenate([raw[0, p], raw[1, p]], axis=0)
        specg[p, 0] = own[:, : width - 1]
        tail = jnp.where(place == p, own[:, width - 1 :].astype(F32), tail)
    last[0] = tail.astype(BF16)

    @pl.when(core == 0)
    def _():
        pl.semaphore_wait(barrier, nlev - 1)
        signal(lev_ready, *sibling)

    @pl.when(core == 1)
    def _():
        pl.semaphore_wait(lev_ready, 1)

    for p in range(pairs):
        for d in sorted(range(1, nx), key=lambda d: -min(d, nx - d)):
            target = 2 * lax.rem(x + d, nx) + core
            if p == 0:
                remote(last.at[0], last.at[d], last_send, last_recv, b, target).start()
            remote(specg.at[p, 0], specg.at[p, d], spec_send, spec_recv.at[p], b, target).start()
        if p == 0:
            loads[1].wait()
        remote(legs.at[p, core], legs.at[p, core], leg_send, leg_recv.at[p], *sibling).start()

    for d in order:
        signal(barrier, lax.rem(b + d, nb), 2 * x + 1)
    after_sums()

    columns = lax.broadcasted_iota(jnp.int32, (16, width - 1), 1)
    zero = jnp.zeros((16, width - 1), F32)
    no_tail = jnp.zeros((16, 1), F32)
    others = last.at[pl.ds(1, nx - 1)]
    remote(others, others, last_send, last_recv, *sibling).wait_recv()
    for p in range(pairs):
        others = specg.at[p, pl.ds(1, nx - 1)]
        remote(others, others, spec_send, spec_recv.at[p], *sibling).wait_recv()
        table_ref = legs.at[p, 0]
        remote(table_ref, table_ref, leg_send, leg_recv.at[p], *sibling).wait_recv()
        first_part = columns < (width - 1 - pair_ref[p])
        parts = []
        for d in range(nx):
            values = specg[p, d].astype(F32)
            tail = last[d].astype(F32)[:, p : p + 1]
            parts.append(jnp.concatenate([jnp.where(first_part, values, zero), no_tail], axis=1))
            parts.append(jnp.concatenate([jnp.where(first_part, zero, values), tail], axis=1))
        rows = jnp.concatenate(parts, axis=0).astype(BF16)
        table = jnp.concatenate([legs[p, 0], legs[p, 1]], axis=0)
        total = nt_dot(rows, table).astype(BF16)
        for d in range(nx):
            sums_out[p, d] = total[d * 32 : (d + 1) * 32]
        sums_in[p, x] = total[:32]
        for d in range(nx - 1, 0, -1):
            remote(
                sums_out.at[p, d],
                sums_in.at[p, x],
                x_send,
                x_recv.at[p],
                b,
                2 * lax.rem(x + nx - d, nx) + core,
            ).start()

    lanes = nx * 32
    lane = lax.broadcasted_iota(jnp.int32, (nb, lanes), 1)
    band = lax.broadcasted_iota(jnp.int32, (nb, lanes), 0)
    numbers = jnp.zeros((nb, lanes), jnp.int32)
    for p in range(pairs):
        numbers = jnp.where(lane == 2 * p, pair_ref[p] // 128, numbers)
        numbers = jnp.where(lane == 2 * p + 1, pair_ref[p] % 128, numbers)
    stage[pl.ds(3 * pairs, nb, stride=16), :] = numbers.astype(F32)
    square = (2 * nb, 2 * nb)
    unit = jnp.where(
        lax.broadcasted_iota(jnp.int32, square, 0) == lax.broadcasted_iota(jnp.int32, square, 1),
        1.0,
        0.0,
    ).astype(BF16)
    before = (lane // 32) % 2 == 0
    outside = ((band == 0) & before) | ((band == nb - 1) & jnp.logical_not(before))
    for p in range(pairs):
        others = sums_out.at[p, pl.ds(1, nx - 1)]
        remote(others, others, x_send, x_recv.at[p], *sibling).wait_recv()
        block = jnp.concatenate([sums_in[p, other] for other in range(nx)], axis=0)
        turned = nt_dot(unit, block)
        low, high = turned[:nb], turned[nb:]
        stage[pl.ds(2 * p, nb, stride=16), :] = low
        stage[pl.ds(2 * p + 1, nb, stride=16), :] = high
        edge = jnp.where(lane < 64, pltpu.roll(low, 32, 1), pltpu.roll(high, 96, 1))
        edge = jnp.where(before, pltpu.roll(edge, 1, 0), pltpu.roll(edge, nb - 1, 0))
        edge = jnp.where(outside, 0.0, edge)
        stage[pl.ds(2 * pairs + p, nb, stride=16), :] = edge
    send[...] = stage[...].reshape(nb, 16, lanes).astype(BF16)
    recv[nb - 1] = send[b]

    @pl.when(core == 1)
    def _():
        pl.semaphore_wait(barrier, 2 * (nb - 1))
        signal(band_ready, *sibling)

    @pl.when(core == 0)
    def _():
        pl.semaphore_wait(band_ready, 1)

    for n, d in enumerate(order):
        target = lax.rem(b + d, nb)
        remote(
            send.at[target], recv.at[n], band_send, band_recv.at[n // group], target, lev
        ).start()

    above = (b, lax.rem(lev + 1, nlev))
    below = (b, lax.rem(lev + nlev - 1, nlev))

    @pl.when(lev == 0)
    def _():
        halo[0] = jnp.zeros(recv.shape, BF16)

    @pl.when(lev == nlev - 1)
    def _():
        halo[1] = jnp.zeros(recv.shape, BF16)

    after_sends()
    for g in reversed(range(GROUPS)):
        end = min(nb - 1, (g + 1) * group)
        if end > g * group:
            arrived = recv.at[pl.ds(g * group, end - g * group)]
            remote(arrived, arrived, band_send, band_recv.at[g], *sibling).wait_recv()
        part = pl.ds(g * group, group)

        @pl.when(lev < nlev - 1)
        def _():
            remote(
                recv.at[part], halo.at[0, part], halo_send.at[0], halo_recv.at[0], *above
            ).start()

        @pl.when(lev > 0)
        def _():
            remote(
                recv.at[part], halo.at[1, part], halo_send.at[1], halo_recv.at[1], *below
            ).start()

    after_own()
    others = last.at[pl.ds(1, nx - 1)]
    remote(others, others, last_send, last_recv, *sibling).wait_send()
    others = specg.at[:, pl.ds(1, nx - 1)]
    remote(others, others, spec_send, spec_recv.at[0], *sibling).wait_send()
    tables = legs.at[:, 0]
    remote(tables, tables, leg_send, leg_recv.at[0], *sibling).wait_send()
    others = sums_out.at[:, pl.ds(1, nx - 1)]
    remote(others, others, x_send, x_recv.at[0], *sibling).wait_send()
    arrived = recv.at[pl.ds(0, nb - 1)]
    remote(arrived, arrived, band_send, band_recv.at[0], *sibling).wait_send()

    up = remote(recv, halo.at[0], halo_send.at[0], halo_recv.at[0], *above)
    down = remote(recv, halo.at[1], halo_send.at[1], halo_recv.at[1], *below)

    @pl.when(lev > 0)
    def _():
        up.wait_recv()
        down.wait_send()

    @pl.when(lev < nlev - 1)
    def _():
        down.wait_recv()
        up.wait_send()


def lagrange_taps(shift, back):
    here = back == 0.0
    x = jnp.clip(back - shift, -0.5, 1.5)
    xm1, xm2, xp1 = x - 1.0, x - 2.0, x + 1.0
    tail = xm1 * xm2
    head = xp1 * x
    first = x * tail * (-1.0 / 6.0)
    second = xp1 * tail * 0.5
    third = head * xm2 * -0.5
    fourth = head * xm1 * (1.0 / 6.0)
    return (
        jnp.where(here, 0.0, first),
        jnp.where(here, first, second),
        jnp.where(here, second, third),
        jnp.where(here, third, fourth),
        jnp.where(here, fourth, 0.0),
    )


def weighted(taps, values):
    total = taps[0] * values[0]
    for tap, value in zip(taps[1:], values[1:]):
        total = total + tap * value
    return total


def whole_kernel(
    nb,
    nx,
    nq,
    pairs,
    width,
    spec_ref,
    leg_ref,
    pair_ref,
    basis_ref,
    eta_ref,
    cells_ref,
    adv_ref,
    disp_ref,
    wide,
    slots,
    place,
    orders,
    coef,
    basis,
    grid,
    near,
    eta,
    cells,
    points,
    eta_wide,
    found,
    adv_wide,
    basis_sem,
    point_sem,
    recv,
    halo,
    *rest,
):
    qp = grid.shape[0] // 8 * 8 // 288
    half = nb * pairs // 2
    window = place.shape[1] // 2
    lon_half = nq * 64
    units = qp // 8
    rows = 8
    row0 = lax.axis_index("band") * rows
    lev0 = lax.axis_index("lev") * 2

    blocks = [(start, min(256, lon_half - start)) for start in range(0, lon_half, 256)]
    basis_copies = [
        pltpu.make_async_copy(
            basis_ref.at[:, :, pl.ds(start, size)],
            basis.at[:, :, pl.ds(start, size)],
            basis_sem.at[n],
        )
        for n, (start, size) in enumerate(blocks)
    ]
    point_copies = (
        pltpu.make_async_copy(eta_ref, eta, point_sem.at[0]),
        pltpu.make_async_copy(cells_ref, cells, point_sem.at[1]),
    )

    def start_copies():
        for copy in (*point_copies, *basis_copies):
            copy.start()

    def read_points():
        for copy in (*point_copies, *basis_copies):
            copy.wait()
        lon = (
            lax.broadcasted_iota(jnp.int32, (nq, 128), 0) * 128
            + lax.broadcasted_iota(jnp.int32, (nq, 128), 1)
        )
        for k in range(2):
            eta_wide[...] = eta[k].astype(F32).reshape(nq * 8, 128)
            for i in range(rows):
                part = pl.ds(i, nq, stride=8)
                at = pl.ds(k * qp, nq)
                points[i, 0, at, :] = jnp.where(cells[0, k, part, :] == row0 + i, 0.0, 1.0)
                points[i, 1, at, :] = jnp.where(cells[1, k, part, :] == lon, 0.0, 1.0)
                points[i, 2, at, :] = jnp.where(cells[2, k, part, :] == lev0 + k, 0.0, 1.0)
                points[i, 3, at, :] = eta_wide[part, :]

    def synthesise(groups, place_of, sums_of):
        first, count = place_of[groups[0]], len(groups)
        for g in groups:
            wide[...] = sums_of[g].astype(F32).reshape(nb * 16, 128)
            for p in range(pairs):
                for t, at in enumerate((2 * p, 2 * p + 1, 2 * pairs + p)):
                    lanes = (place_of[g] * 3 + t) * 128
                    slots[p * nb : (p + 1) * nb, lanes : lanes + 128] = wide[
                        pl.ds(at, nb, stride=16), :
                    ].astype(BF16)
            if g == 1:
                numbers = wide[pl.ds(3 * pairs, nb, stride=16), :].astype(jnp.int32)
                column = lax.broadcasted_iota(jnp.int32, (nb, 2 * window), 1)
                order = jnp.where(column < window, 2 * column, 2 * (column - window) + 1)
                for p in range(pairs):
                    number = (
                        numbers[:, 2 * p : 2 * p + 1] * 128 + numbers[:, 2 * p + 1 : 2 * p + 2]
                    )
                    place[p * nb : (p + 1) * nb, :] = jnp.where(order == number, 1.0, 0.0).astype(
                        BF16
                    )
        used = slots[:, first * 384 : (first + count) * 384]
        orders[first * 48 : (first + count) * 48] = tn_dot(used, place[...]).reshape(
            count * 48, 8, 2 * window
        )
        lines = pl.ds(first * 96, count * 96)
        for parity in range(2):
            for part in range(4):
                start = window * ((part // 2 + parity) % 2)
                coef[parity, part, lines, :] = jnp.concatenate(
                    [
                        orders[first * 48 + 4 * m + part, :, start : start + window]
                        for m in range(12 * count)
                    ],
                    axis=0,
                ).astype(BF16)
        for start, size in blocks:
            even, odd = [
                sum(
                    jnp.dot(
                        coef[parity, part, lines, :half],
                        basis[parity, part * half : (part + 1) * half, start : start + size],
                        preferred_element_type=F32,
                    )
                    for part in range(4)
                )
                for parity in range(2)
            ]
            for turn, values in enumerate((even + odd, even - odd)):
                for m in range(12 * count):
                    g, t, xs = groups[m // 12], (m // 4) % 3, m % 4
                    row = 2 + 2 * xs + t if t < 2 else (xs // 2 + (xs % 2) * 10)
                    base = (row * 3 + g) * 8 * qp + 1 + (start + turn * lon_half) // 128
                    for w in range(size // 128):
                        grid[pl.ds(base + w, 8, stride=qp), :] = values[
                            m * 8 : (m + 1) * 8, w * 128 : (w + 1) * 128
                        ]

    place_of = (1, 0, 2)

    def own_levels():
        synthesise((1,), place_of, {1: recv[...]})

    gather_sums(
        nb,
        nx,
        pairs,
        width,
        start_copies,
        read_points,
        own_levels,
        spec_ref,
        leg_ref,
        pair_ref,
        recv,
        halo,
        *rest,
    )
    synthesise((0, 2), place_of, {0: halo[0], 2: halo[1]})
    grid[pl.ds(0, 288, stride=qp), :] = grid[pl.ds(nq, 288, stride=qp), :]
    grid[pl.ds(nq + 1, 288, stride=qp), :] = grid[pl.ds(1, 288, stride=qp), :]

    lane = lax.broadcasted_iota(jnp.int32, (16, 128), 1).astype(F32).astype(TAP)
    inside = {c: (lane >= c if c > 0 else lane < 128 + c) for c in (-2, -1, 1, 2)}

    def shift_fields(n, carry):
        row, level = n // 6, n % 6
        for two in range(2):
            for t in range(units):

                def block(offset):
                    return jnp.concatenate(
                        [
                            grid[pl.ds((n * 4 + field) * qp + 8 * t + offset, 8), :]
                            for field in (2 * two, 2 * two + 1)
                        ],
                        axis=0,
                    ).astype(TAP)

                ahead, here, after = block(0), block(1), block(2)
                for c in range(-2, 3):
                    value = here
                    if c > 0:
                        value = pltpu.roll(jnp.where(inside[c], here, after), 128 - c, 1)
                    elif c < 0:
                        value = pltpu.roll(jnp.where(inside[c], here, ahead), -c, 1)
                    near[row, level, t, two, c + 2] = value
        return carry

    lax.fori_loop(0, 72, shift_fields, 0, unroll=8)

    def double(taps):
        return [jnp.concatenate([tap, tap], axis=0).astype(TAP) for tap in taps]

    def depart(n, carry):
        i, k, t = n // (2 * units), (n // units) % 2, n % units
        at = pl.ds(pl.multiple_of((k * units + t) * 8, 8), 8)
        row_back, lon_back = points[i, 0, at, :], points[i, 1, at, :]
        level_taps = double(lagrange_taps(points[i, 3, at, :], points[i, 2, at, :]))

        def level_sums(two):
            return [
                [
                    weighted(level_taps, [near[i + b, k + a, t, two, c] for a in range(5)])
                    for c in range(5)
                ]
                for b in range(5)
            ]

        def horizontal(sums, shift_row, shift_lon):
            row_taps = lagrange_taps(shift_row, row_back)
            lon_taps = double(lagrange_taps(shift_lon, lon_back))
            lines = [weighted(lon_taps, sums[b]).astype(F32) for b in range(5)]
            return [
                weighted(row_taps, [line[s * 8 : (s + 1) * 8] for line in lines]) for s in range(2)
            ]

        wind = near[i + 2, k + 2, t, 0, 2].astype(F32)
        east, north = wind[:8], wind[8:]
        wind_sums = level_sums(0)
        shift_row, shift_lon = COURANT * north, COURANT * east
        for sweep in range(ITERS):
            east_found, north_found = horizontal(wind_sums, shift_row, shift_lon)
            shift_row = 0.5 * COURANT * (north + north_found)
            shift_lon = 0.5 * COURANT * (east + east_found)
        found[i, 0, at, :] = shift_row
        found[i, 1, at, :] = shift_lon
        heat, moisture = horizontal(level_sums(1), shift_row, shift_lon)
        found[i, 2, at, :] = heat
        found[i, 3, at, :] = moisture
        return carry

    lax.fori_loop(0, rows * 2 * units, depart, 0, unroll=4)
    for k in range(2):
        for i in range(rows):
            part = pl.ds(i, nq, stride=8)
            at = pl.ds(k * qp, nq)
            for which in range(2):
                disp_ref[which, k, part, :] = found[i, which, at, :]
                adv_wide[which, k, part, :] = found[i, 2 + which, at, :]
    adv_ref[...] = adv_wide[...].reshape(adv_ref.shape).astype(BF16)


def basis_table(total, lon_total):
    npairs = total // 2
    m = np.arange(npairs // 2, dtype=np.int64)
    j = np.arange(lon_total // 2, dtype=np.int64)
    orders = ((2 * m, total - 2 - 2 * m), (2 * m + 1, total - 1 - 2 * m))
    table = np.zeros((2, 2, 2, npairs // 2, lon_total // 2), np.float32)
    for parity in range(2):
        for half in range(2):
            order = orders[parity][half][:, None]
            angle = (2.0 * math.pi / lon_total) * ((order * j[None, :]) % lon_total)
            weight = np.where(order == 0, 1.0, 2.0)
            table[parity, half, 0] = weight * np.cos(angle)
            table[parity, half, 1] = -weight * np.sin(angle)
    return jnp.asarray(table.reshape(2, 2 * npairs, lon_total // 2).astype(BF16))


def hand_over(adv_ref, disp_ref, adv_out, disp_out):
    adv_out[...] = adv_ref[...]
    disp_out[...] = disp_ref[...]


def per_device(spectra, legendre, pairing, eta_shift, cells):
    nb = legendre.shape[1]
    pairs, width = spectra.shape[2], spectra.shape[3]
    nx = lax.axis_size("lev") // 2
    lon_total = eta_shift.shape[2]
    nq = lon_total // 128
    qp = -(-(nq + 2) // 8) * 8
    basis = basis_table(width - 1, lon_total)
    window = -(-(width - 1) // 4 // 128) * 128
    tiles = lambda a: jnp.swapaxes(a.reshape(a.shape[:-1] + (nq, 128)), -3, -2)
    eta = tiles(eta_shift)
    cells = tiles(cells).reshape(3, 2, nq * 8, 128)
    spec = jnp.transpose(spectra, (0, 2, 1, 3))
    table = jnp.transpose(legendre[0], (1, 0, 2))
    lanes = nx * 32
    dma = pltpu.SemaphoreType.DMA
    regular = pltpu.SemaphoreType.REGULAR
    vmem = pl.BlockSpec(memory_space=pltpu.VMEM)
    anywhere = pl.BlockSpec(memory_space=pl.ANY)
    adv, disp = pl.pallas_call(
        functools.partial(whole_kernel, nb, nx, nq, pairs, width),
        out_shape=(
            jax.ShapeDtypeStruct((2, 2, nq, 8, 128), BF16),
            jax.ShapeDtypeStruct((2, 2, nq * 8, 128), F32),
        ),
        in_specs=[anywhere, anywhere, pl.BlockSpec(memory_space=pltpu.SMEM)] + [anywhere] * 3,
        out_specs=(vmem, vmem),
        scratch_shapes=[
            pltpu.VMEM((nb * 16, 128), F32),
            pltpu.VMEM((nb * pairs, 9 * 128), BF16),
            pltpu.VMEM((nb * pairs, 2 * window), BF16),
            pltpu.VMEM((144, 8, 2 * window), F32),
            pltpu.VMEM((2, 4, 288, window), BF16),
            pltpu.VMEM(basis.shape, BF16),
            pltpu.VMEM((288 * qp + 8, 128), F32),
            pltpu.VMEM((12, 6, qp // 8, 2, 5, 16, 128), TAP),
            pltpu.VMEM(eta.shape, BF16),
            pltpu.VMEM(cells.shape, jnp.int32),
            pltpu.VMEM((8, 4, 2 * qp, 128), F32),
            pltpu.VMEM((nq * 8, 128), F32),
            pltpu.VMEM((8, 4, 2 * qp, 128), F32),
            pltpu.VMEM((2, 2, nq * 8, 128), F32),
            dma((-(-lon_total // 512),)),
            dma((2,)),
            pltpu.VMEM((nb, 16, lanes), BF16),
            pltpu.VMEM((2, nb, 16, lanes), BF16),
            pltpu.VMEM(spec.shape, BF16),
            pltpu.VMEM((pairs, nx, 16, width - 1), BF16),
            pltpu.VMEM((nx, 16, 128), BF16),
            pltpu.VMEM((pairs, 2, nb, width), BF16),
            pltpu.VMEM((pairs, nx, 32, 2 * nb), BF16),
            pltpu.VMEM((pairs, nx, 32, 2 * nb), BF16),
            pltpu.VMEM((nb * 16, lanes), F32),
            pltpu.VMEM((nb, 16, lanes), BF16),
            dma((2,)),
            dma,
            dma,
            dma,
            dma((pairs,)),
            dma,
            dma((pairs,)),
            dma,
            dma((pairs,)),
            dma,
            dma((GROUPS,)),
            dma((2,)),
            dma((2,)),
            regular,
            regular,
        ],
        compiler_params=pltpu.CompilerParams(
            collective_id=0, has_side_effects=True, vmem_limit_bytes=VMEM_LIMIT
        ),
        name="winds",
    )(spec, table, pairing, basis, eta, cells)
    adv, disp = pl.pallas_call(
        hand_over,
        out_shape=(
            jax.ShapeDtypeStruct(adv.shape, adv.dtype),
            jax.ShapeDtypeStruct(disp.shape, disp.dtype),
        ),
        in_specs=[vmem] * 2,
        out_specs=(vmem, vmem),
        name="results",
    )(adv, disp)
    whole = lambda a: jnp.swapaxes(a, -3, -2).reshape(2, 2, 8, lon_total)
    return whole(adv), whole(disp.reshape(2, 2, nq, 8, 128))


def solution(mesh):
    return jax.shard_map(
        per_device,
        mesh=mesh,
        in_specs=(
            P(None, "lev", "band", None),
            P("lev", None, "band", None),
            P("band"),
            P("lev", "band", None),
            P(None, "lev", "band", None),
        ),
        out_specs=(P(None, "lev", "band", None), P(None, "lev", "band", None)),
        check_vma=False,
    )
```

```python
import functools
import math

import jax
import jax.numpy as jnp
import numpy as np
from jax import lax
from jax.experimental import pallas as pl
from jax.experimental.pallas import tpu as pltpu
from jax.sharding import PartitionSpec as P

ITERS = 2
COURANT = 0.8
MESH = pl.DeviceIdType.MESH
BF16 = jnp.bfloat16
F32 = jnp.float32
TAP = jnp.bfloat16
VMEM_LIMIT = 60 * 1024 * 1024
GROUPS = 8


def nt_dot(a, b):
    return lax.dot_general(a, b, (((1,), (1,)), ((), ())), preferred_element_type=F32)


def tn_dot(a, b):
    return lax.dot_general(a, b, (((0,), (0,)), ((), ())), preferred_element_type=F32)


def gather_sums(
    nb,
    nx,
    pairs,
    width,
    after_sums,
    after_sends,
    after_own,
    spec_ref,
    leg_ref,
    pair_ref,
    recv,
    halo,
    raw,
    specg,
    last,
    legs,
    sums_out,
    sums_in,
    stage,
    send,
    load_sem,
    last_send,
    last_recv,
    spec_send,
    spec_recv,
    leg_send,
    leg_recv,
    x_send,
    x_recv,
    band_send,
    band_recv,
    halo_send,
    halo_recv,
    lev_ready,
    band_ready,
):
    b = lax.axis_index("band")
    lev = lax.axis_index("lev")
    nlev = 2 * nx
    x = lev // 2
    core = lev % 2
    group = max(1, nb // GROUPS)

    def remote(src, dst, send_sem, recv_sem, band, level):
        return pltpu.make_async_remote_copy(
            src_ref=src,
            dst_ref=dst,
            send_sem=send_sem,
            recv_sem=recv_sem,
            device_id=(band, level),
            device_id_type=MESH,
        )

    def signal(semaphore, band, level):
        pl.semaphore_signal(semaphore, inc=1, device_id=(band, level), device_id_type=MESH)

    side = math.isqrt(nb)

    def hops(d):
        return sum(min(n, side - n) for n in (d // side, d % side))

    order = sorted(range(1, nb), key=lambda d: -hops(d))
    sibling = (b, 2 * x + 1 - core)

    loads = (
        pltpu.make_async_copy(spec_ref, raw, load_sem.at[0]),
        pltpu.make_async_copy(leg_ref, legs.at[:, core], load_sem.at[1]),
    )
    for load in loads:
        load.start()
    barrier = pltpu.get_barrier_semaphore()

    for d in range(1, nx):
        signal(barrier, b, 2 * lax.rem(x + d, nx))

    @pl.when(core == 1)
    def _():
        signal(barrier, b, 2 * x)

    for d in order:
        signal(barrier, lax.rem(b + d, nb), 2 * x + 1)
    loads[0].wait()
    tail = jnp.zeros((16, 128), F32)
    place = lax.broadcasted_iota(jnp.int32, (16, 128), 1)
    for p in range(pairs):
        own = jnp.concatenate([raw[0, p], raw[1, p]], axis=0)
        specg[p, 0] = own[:, : width - 1]
        tail = jnp.where(place == p, own[:, width - 1 :].astype(F32), tail)
    last[0] = tail.astype(BF16)

    @pl.when(core == 0)
    def _():
        pl.semaphore_wait(barrier, nlev - 1)
        signal(lev_ready, *sibling)

    @pl.when(core == 1)
    def _():
        pl.semaphore_wait(lev_ready, 1)

    for p in range(pairs):
        for d in sorted(range(1, nx), key=lambda d: -min(d, nx - d)):
            target = 2 * lax.rem(x + d, nx) + core
            if p == 0:
                remote(last.at[0], last.at[d], last_send, last_recv, b, target).start()
            remote(specg.at[p, 0], specg.at[p, d], spec_send, spec_recv.at[p], b, target).start()
        if p == 0:
            loads[1].wait()
        remote(legs.at[p, core], legs.at[p, core], leg_send, leg_recv.at[p], *sibling).start()

    after_sums()

    columns = lax.broadcasted_iota(jnp.int32, (16, width - 1), 1)
    zero = jnp.zeros((16, width - 1), F32)
    no_tail = jnp.zeros((16, 1), F32)
    others = last.at[pl.ds(1, nx - 1)]
    remote(others, others, last_send, last_recv, *sibling).wait_recv()
    for p in range(pairs):
        others = specg.at[p, pl.ds(1, nx - 1)]
        remote(others, others, spec_send, spec_recv.at[p], *sibling).wait_recv()
        table_ref = legs.at[p, 0]
        remote(table_ref, table_ref, leg_send, leg_recv.at[p], *sibling).wait_recv()
        first_part = columns < (width - 1 - pair_ref[p])
        parts = []
        for d in range(nx):
            values = specg[p, d].astype(F32)
            tail = last[d].astype(F32)[:, p : p + 1]
            parts.append(jnp.concatenate([jnp.where(first_part, values, zero), no_tail], axis=1))
            parts.append(jnp.concatenate([jnp.where(first_part, zero, values), tail], axis=1))
        rows = jnp.concatenate(parts, axis=0).astype(BF16)
        table = jnp.concatenate([legs[p, 0], legs[p, 1]], axis=0)
        total = nt_dot(rows, table).astype(BF16)
        for d in range(nx):
            sums_out[p, d] = total[d * 32 : (d + 1) * 32]
        sums_in[p, x] = total[:32]
        for d in range(nx - 1, 0, -1):
            remote(
                sums_out.at[p, d],
                sums_in.at[p, x],
                x_send,
                x_recv.at[p],
                b,
                2 * lax.rem(x + nx - d, nx) + core,
            ).start()

    lanes = nx * 32
    lane = lax.broadcasted_iota(jnp.int32, (nb, lanes), 1)
    band = lax.broadcasted_iota(jnp.int32, (nb, lanes), 0)
    numbers = jnp.zeros((nb, lanes), jnp.int32)
    for p in range(pairs):
        numbers = jnp.where(lane == 2 * p, pair_ref[p] // 128, numbers)
        numbers = jnp.where(lane == 2 * p + 1, pair_ref[p] % 128, numbers)
    stage[pl.ds(3 * pairs, nb, stride=16), :] = numbers.astype(F32)
    square = (2 * nb, 2 * nb)
    unit = jnp.where(
        lax.broadcasted_iota(jnp.int32, square, 0) == lax.broadcasted_iota(jnp.int32, square, 1),
        1.0,
        0.0,
    ).astype(BF16)
    before = (lane // 32) % 2 == 0
    outside = ((band == 0) & before) | ((band == nb - 1) & jnp.logical_not(before))
    for p in range(pairs):
        others = sums_out.at[p, pl.ds(1, nx - 1)]
        remote(others, others, x_send, x_recv.at[p], *sibling).wait_recv()
        block = jnp.concatenate([sums_in[p, other] for other in range(nx)], axis=0)
        turned = nt_dot(unit, block)
        low, high = turned[:nb], turned[nb:]
        stage[pl.ds(2 * p, nb, stride=16), :] = low
        stage[pl.ds(2 * p + 1, nb, stride=16), :] = high
        edge = jnp.where(lane < 64, pltpu.roll(low, 32, 1), pltpu.roll(high, 96, 1))
        edge = jnp.where(before, pltpu.roll(edge, 1, 0), pltpu.roll(edge, nb - 1, 0))
        edge = jnp.where(outside, 0.0, edge)
        stage[pl.ds(2 * pairs + p, nb, stride=16), :] = edge
    send[...] = stage[...].reshape(nb, 16, lanes).astype(BF16)
    recv[nb - 1] = send[b]

    @pl.when(core == 1)
    def _():
        pl.semaphore_wait(barrier, 2 * (nb - 1))
        signal(band_ready, *sibling)

    @pl.when(core == 0)
    def _():
        pl.semaphore_wait(band_ready, 1)

    for n, d in enumerate(order):
        target = lax.rem(b + d, nb)
        remote(
            send.at[target], recv.at[n], band_send, band_recv.at[n // group], target, lev
        ).start()

    above = (b, lax.rem(lev + 1, nlev))
    below = (b, lax.rem(lev + nlev - 1, nlev))

    @pl.when(lev == 0)
    def _():
        halo[0] = jnp.zeros(recv.shape, BF16)

    @pl.when(lev == nlev - 1)
    def _():
        halo[1] = jnp.zeros(recv.shape, BF16)

    after_sends()
    for g in reversed(range(GROUPS)):
        end = min(nb - 1, (g + 1) * group)
        if end > g * group:
            arrived = recv.at[pl.ds(g * group, end - g * group)]
            remote(arrived, arrived, band_send, band_recv.at[g], *sibling).wait_recv()
        part = pl.ds(g * group, group)

        @pl.when(lev < nlev - 1)
        def _():
            remote(
                recv.at[part], halo.at[0, part], halo_send.at[0], halo_recv.at[0], *above
            ).start()

        @pl.when(lev > 0)
        def _():
            remote(
                recv.at[part], halo.at[1, part], halo_send.at[1], halo_recv.at[1], *below
            ).start()

    after_own()
    others = last.at[pl.ds(1, nx - 1)]
    remote(others, others, last_send, last_recv, *sibling).wait_send()
    others = specg.at[:, pl.ds(1, nx - 1)]
    remote(others, others, spec_send, spec_recv.at[0], *sibling).wait_send()
    tables = legs.at[:, 0]
    remote(tables, tables, leg_send, leg_recv.at[0], *sibling).wait_send()
    others = sums_out.at[:, pl.ds(1, nx - 1)]
    remote(others, others, x_send, x_recv.at[0], *sibling).wait_send()
    arrived = recv.at[pl.ds(0, nb - 1)]
    remote(arrived, arrived, band_send, band_recv.at[0], *sibling).wait_send()

    up = remote(recv, halo.at[0], halo_send.at[0], halo_recv.at[0], *above)
    down = remote(recv, halo.at[1], halo_send.at[1], halo_recv.at[1], *below)

    @pl.when(lev > 0)
    def _():
        up.wait_recv()
        down.wait_send()

    @pl.when(lev < nlev - 1)
    def _():
        down.wait_recv()
        up.wait_send()


def lagrange_taps(shift, back):
    here = back == 0.0
    x = jnp.clip(back - shift, -0.5, 1.5)
    xm1, xm2, xp1 = x - 1.0, x - 2.0, x + 1.0
    tail = xm1 * xm2
    head = xp1 * x
    first = x * tail * (-1.0 / 6.0)
    second = xp1 * tail * 0.5
    third = head * xm2 * -0.5
    fourth = head * xm1 * (1.0 / 6.0)
    return (
        jnp.where(here, 0.0, first),
        jnp.where(here, first, second),
        jnp.where(here, second, third),
        jnp.where(here, third, fourth),
        jnp.where(here, fourth, 0.0),
    )


def weighted(taps, values):
    total = taps[0] * values[0]
    for tap, value in zip(taps[1:], values[1:]):
        total = total + tap * value
    return total


def whole_kernel(
    nb,
    nx,
    nq,
    pairs,
    width,
    spec_ref,
    leg_ref,
    pair_ref,
    basis_ref,
    eta_ref,
    cells_ref,
    adv_ref,
    disp_ref,
    wide,
    slots,
    place,
    orders,
    coef,
    basis,
    grid,
    near,
    eta,
    cells,
    points,
    eta_wide,
    disp,
    adv_wide,
    adv,
    basis_sem,
    point_sem,
    out_sem,
    recv,
    halo,
    *rest,
):
    qp = grid.shape[0] // 8 * 8 // 288
    half = nb * pairs // 2
    window = place.shape[1] // 2
    lon_half = nq * 64
    units = qp // 8
    rows = 8
    row0 = lax.axis_index("band") * rows
    lev0 = lax.axis_index("lev") * 2

    blocks = [(start, min(256, lon_half - start)) for start in range(0, lon_half, 256)]
    basis_copies = [
        pltpu.make_async_copy(
            basis_ref.at[:, :, pl.ds(start, size)],
            basis.at[:, :, pl.ds(start, size)],
            basis_sem.at[n],
        )
        for n, (start, size) in enumerate(blocks)
    ]
    point_copies = (
        pltpu.make_async_copy(eta_ref, eta, point_sem.at[0]),
        pltpu.make_async_copy(cells_ref, cells, point_sem.at[1]),
    )

    def start_copies():
        for copy in (*point_copies, *basis_copies):
            copy.start()

    def read_points():
        for copy in (*point_copies, *basis_copies):
            copy.wait()
        lon = (
            lax.broadcasted_iota(jnp.int32, (nq, 128), 0) * 128
            + lax.broadcasted_iota(jnp.int32, (nq, 128), 1)
        )
        for k in range(2):
            eta_wide[...] = eta[k].astype(F32).reshape(nq * 8, 128)
            for i in range(rows):
                part = pl.ds(i, nq, stride=8)
                at = pl.ds(k * qp, nq)
                points[i, 0, at, :] = jnp.where(cells[0, k, part, :] == row0 + i, 0.0, 1.0)
                points[i, 1, at, :] = jnp.where(cells[1, k, part, :] == lon, 0.0, 1.0)
                points[i, 2, at, :] = jnp.where(cells[2, k, part, :] == lev0 + k, 0.0, 1.0)
                points[i, 3, at, :] = eta_wide[part, :]

    lane = lax.broadcasted_iota(jnp.int32, (16, 128), 1).astype(F32).astype(TAP)
    inside = {c: (lane >= c if c > 0 else lane < 128 + c) for c in (-2, -1, 1, 2)}

    def shift_fields(first, count, n, carry):
        row, level = n // count, first + n % count
        if count == 4:
            level = level + 2 * (n % count // 2)
        at = (row * 6 + level) * 4
        for two in range(2):
            for t in range(units):

                def block(offset):
                    return jnp.concatenate(
                        [
                            grid[pl.ds((at + field) * qp + 8 * t + offset, 8), :]
                            for field in (2 * two, 2 * two + 1)
                        ],
                        axis=0,
                    ).astype(TAP)

                ahead, here, after = block(0), block(1), block(2)
                for c in range(-2, 3):
                    value = here
                    if c > 0:
                        value = pltpu.roll(jnp.where(inside[c], here, after), 128 - c, 1)
                    elif c < 0:
                        value = pltpu.roll(jnp.where(inside[c], here, ahead), -c, 1)
                    near[row, level, t, two, c + 2] = value
        return carry

    def synthesise(groups, place_of, sums_of):
        first, count = place_of[groups[0]], len(groups)
        for g in groups:
            wide[...] = sums_of[g].astype(F32).reshape(nb * 16, 128)
            for p in range(pairs):
                for t, at in enumerate((2 * p, 2 * p + 1, 2 * pairs + p)):
                    lanes = (place_of[g] * 3 + t) * 128
                    slots[p * nb : (p + 1) * nb, lanes : lanes + 128] = wide[
                        pl.ds(at, nb, stride=16), :
                    ].astype(BF16)
            if g == 1:
                numbers = wide[pl.ds(3 * pairs, nb, stride=16), :].astype(jnp.int32)
                column = lax.broadcasted_iota(jnp.int32, (nb, 2 * window), 1)
                order = jnp.where(column < window, 2 * column, 2 * (column - window) + 1)
                for p in range(pairs):
                    number = (
                        numbers[:, 2 * p : 2 * p + 1] * 128 + numbers[:, 2 * p + 1 : 2 * p + 2]
                    )
                    place[p * nb : (p + 1) * nb, :] = jnp.where(order == number, 1.0, 0.0).astype(
                        BF16
                    )
        used = slots[:, first * 384 : (first + count) * 384]
        orders[first * 48 : (first + count) * 48] = tn_dot(used, place[...]).reshape(
            count * 48, 8, 2 * window
        )
        lines = pl.ds(first * 96, count * 96)
        for parity in range(2):
            for part in range(4):
                start = window * ((part // 2 + parity) % 2)
                coef[parity, part, lines, :] = jnp.concatenate(
                    [
                        orders[first * 48 + 4 * m + part, :, start : start + window]
                        for m in range(12 * count)
                    ],
                    axis=0,
                ).astype(BF16)
        for start, size in blocks:
            even, odd = [
                sum(
                    jnp.dot(
                        coef[parity, part, lines, :half],
                        basis[parity, part * half : (part + 1) * half, start : start + size],
                        preferred_element_type=F32,
                    )
                    for part in range(4)
                )
                for parity in range(2)
            ]
            for turn, values in enumerate((even + odd, even - odd)):
                for m in range(12 * count):
                    g, t, xs = groups[m // 12], (m // 4) % 3, m % 4
                    row = 2 + 2 * xs + t if t < 2 else (xs // 2 + (xs % 2) * 10)
                    base = (row * 3 + g) * 8 * qp + 1 + (start + turn * lon_half) // 128
                    for w in range(size // 128):
                        grid[pl.ds(base + w, 8, stride=qp), :] = values[
                            m * 8 : (m + 1) * 8, w * 128 : (w + 1) * 128
                        ]
        for row in range(12):
            for g in groups:
                base = (row * 3 + g) * 8 * qp
                for target, source in ((0, nq), (nq + 1, 1)):
                    grid[pl.ds(base + target, 8, stride=qp), :] = grid[
                        pl.ds(base + source, 8, stride=qp), :
                    ]
        shift = functools.partial(shift_fields, 2 * groups[0], 2 * count)
        lax.fori_loop(0, 24 * count, shift, 0, unroll=12)

    place_of = (1, 0, 2)

    def own_levels():
        synthesise((1,), place_of, {1: recv[...]})

    gather_sums(
        nb,
        nx,
        pairs,
        width,
        start_copies,
        read_points,
        own_levels,
        spec_ref,
        leg_ref,
        pair_ref,
        recv,
        halo,
        *rest,
    )
    synthesise((0, 2), place_of, {0: halo[0], 2: halo[1]})
    def double(taps):
        return [jnp.concatenate([tap, tap], axis=0).astype(TAP) for tap in taps]

    def depart(k, t, i, carry):
        at = pl.ds(pl.multiple_of((k * units + t) * 8, 8), 8)
        row_back, lon_back = points[i, 0, at, :], points[i, 1, at, :]
        level_taps = double(lagrange_taps(points[i, 3, at, :], points[i, 2, at, :]))

        def level_sums(two):
            return [
                [
                    weighted(level_taps, [near[i + b, k + a, t, two, c] for a in range(5)])
                    for c in range(5)
                ]
                for b in range(5)
            ]

        def horizontal(sums, shift_row, shift_lon):
            row_taps = lagrange_taps(shift_row, row_back)
            lon_taps = double(lagrange_taps(shift_lon, lon_back))
            lines = [weighted(lon_taps, sums[b]).astype(F32) for b in range(5)]
            return [
                weighted(row_taps, [line[s * 8 : (s + 1) * 8] for line in lines]) for s in range(2)
            ]

        wind = near[i + 2, k + 2, t, 0, 2].astype(F32)
        east, north = wind[:8], wind[8:]
        wind_sums = level_sums(0)
        shift_row, shift_lon = COURANT * north, COURANT * east
        for sweep in range(ITERS):
            east_found, north_found = horizontal(wind_sums, shift_row, shift_lon)
            shift_row = 0.5 * COURANT * (north + north_found)
            shift_lon = 0.5 * COURANT * (east + east_found)
        heat, moisture = horizontal(level_sums(1), shift_row, shift_lon)
        out = pl.ds(t * 64 + i, 8, stride=8)
        disp[0, k, out, :] = shift_row
        disp[1, k, out, :] = shift_lon
        adv_wide[0, k, out, :] = heat
        adv_wide[1, k, out, :] = moisture
        return carry

    def results(k, t, size):
        for which in range(2):
            blocks = pl.ds(t * 8, size)
            lines = pl.ds(pl.multiple_of(t * 64, 64), size * 8)
            adv[which, k, blocks] = (
                adv_wide[which, k, lines, :].reshape(size, 8, 128).astype(BF16)
            )
            pltpu.make_async_copy(
                adv.at[which, k, blocks], adv_ref.at[which, k, blocks], out_sem.at[0]
            ).start()
            pltpu.make_async_copy(
                disp.at[which, k, lines], disp_ref.at[which, k, lines], out_sem.at[1]
            ).start()

    def depart_block(n, carry):
        k, t = n // units, n % units
        lax.fori_loop(0, rows, functools.partial(depart, k, t), 0, unroll=8)

        @pl.when(t < units - 1)
        def _():
            results(k, t, 8)

        @pl.when(t == units - 1)
        def _():
            results(k, t, nq - 8 * (units - 1))

        return carry

    lax.fori_loop(0, 2 * units, depart_block, 0)
    pltpu.make_async_copy(adv.at[:, :, pl.ds(0, nq)], adv_ref, out_sem.at[0]).wait()
    pltpu.make_async_copy(disp.at[:, :, pl.ds(0, nq * 8)], disp_ref, out_sem.at[1]).wait()


def basis_table(total, lon_total):
    npairs = total // 2
    m = np.arange(npairs // 2, dtype=np.int64)
    j = np.arange(lon_total // 2, dtype=np.int64)
    orders = ((2 * m, total - 2 - 2 * m), (2 * m + 1, total - 1 - 2 * m))
    table = np.zeros((2, 2, 2, npairs // 2, lon_total // 2), np.float32)
    for parity in range(2):
        for half in range(2):
            order = orders[parity][half][:, None]
            angle = (2.0 * math.pi / lon_total) * ((order * j[None, :]) % lon_total)
            weight = np.where(order == 0, 1.0, 2.0)
            table[parity, half, 0] = weight * np.cos(angle)
            table[parity, half, 1] = -weight * np.sin(angle)
    return jnp.asarray(table.reshape(2, 2 * npairs, lon_total // 2).astype(BF16))


def hand_over(adv_ref, disp_ref, adv_out, disp_out, adv, disp, in_sem, out_sem):
    steps = []
    for n, (source, held, target) in enumerate(
        ((disp_ref, disp, disp_out), (adv_ref, adv, adv_out))
    ):
        for which in range(2):
            for k in range(2):
                at = (n, which, k)
                inward = pltpu.make_async_copy(
                    source.at[which, k], held.at[which, k], in_sem.at[at]
                )
                outward = pltpu.make_async_copy(
                    held.at[which, k], target.at[which, k], out_sem.at[at]
                )
                inward.start()
                steps.append((inward, outward))
    for inward, outward in steps:
        inward.wait()
        outward.start()
    for inward, outward in steps:
        outward.wait()


def per_device(spectra, legendre, pairing, eta_shift, cells):
    nb = legendre.shape[1]
    pairs, width = spectra.shape[2], spectra.shape[3]
    nx = lax.axis_size("lev") // 2
    lon_total = eta_shift.shape[2]
    nq = lon_total // 128
    qp = -(-(nq + 2) // 8) * 8
    basis = basis_table(width - 1, lon_total)
    window = -(-(width - 1) // 4 // 128) * 128
    tiles = lambda a: jnp.swapaxes(a.reshape(a.shape[:-1] + (nq, 128)), -3, -2)
    eta = tiles(eta_shift)
    cells = tiles(cells).reshape(3, 2, nq * 8, 128)
    spec = jnp.transpose(spectra, (0, 2, 1, 3))
    table = jnp.transpose(legendre[0], (1, 0, 2))
    lanes = nx * 32
    dma = pltpu.SemaphoreType.DMA
    regular = pltpu.SemaphoreType.REGULAR
    anywhere = pl.BlockSpec(memory_space=pl.ANY)
    adv, disp = pl.pallas_call(
        functools.partial(whole_kernel, nb, nx, nq, pairs, width),
        out_shape=(
            jax.ShapeDtypeStruct((2, 2, nq, 8, 128), BF16),
            jax.ShapeDtypeStruct((2, 2, nq * 8, 128), F32),
        ),
        in_specs=[anywhere, anywhere, pl.BlockSpec(memory_space=pltpu.SMEM)] + [anywhere] * 3,
        out_specs=(anywhere, anywhere),
        scratch_shapes=[
            pltpu.VMEM((nb * 16, 128), F32),
            pltpu.VMEM((nb * pairs, 9 * 128), BF16),
            pltpu.VMEM((nb * pairs, 2 * window), BF16),
            pltpu.VMEM((144, 8, 2 * window), F32),
            pltpu.VMEM((2, 4, 288, window), BF16),
            pltpu.VMEM(basis.shape, BF16),
            pltpu.VMEM((288 * qp + 8, 128), F32),
            pltpu.VMEM((12, 6, qp // 8, 2, 5, 16, 128), TAP),
            pltpu.VMEM(eta.shape, BF16),
            pltpu.VMEM(cells.shape, jnp.int32),
            pltpu.VMEM((8, 4, 2 * qp, 128), F32),
            pltpu.VMEM((nq * 8, 128), F32),
            pltpu.VMEM((2, 2, qp * 8, 128), F32),
            pltpu.VMEM((2, 2, qp * 8, 128), F32),
            pltpu.VMEM((2, 2, qp, 8, 128), BF16),
            dma((-(-lon_total // 512),)),
            dma((2,)),
            dma((2,)),
            pltpu.VMEM((nb, 16, lanes), BF16),
            pltpu.VMEM((2, nb, 16, lanes), BF16),
            pltpu.VMEM(spec.shape, BF16),
            pltpu.VMEM((pairs, nx, 16, width - 1), BF16),
            pltpu.VMEM((nx, 16, 128), BF16),
            pltpu.VMEM((pairs, 2, nb, width), BF16),
            pltpu.VMEM((pairs, nx, 32, 2 * nb), BF16),
            pltpu.VMEM((pairs, nx, 32, 2 * nb), BF16),
            pltpu.VMEM((nb * 16, lanes), F32),
            pltpu.VMEM((nb, 16, lanes), BF16),
            dma((2,)),
            dma,
            dma,
            dma,
            dma((pairs,)),
            dma,
            dma((pairs,)),
            dma,
            dma((pairs,)),
            dma,
            dma((GROUPS,)),
            dma((2,)),
            dma((2,)),
            regular,
            regular,
        ],
        compiler_params=pltpu.CompilerParams(
            collective_id=0, has_side_effects=True, vmem_limit_bytes=VMEM_LIMIT
        ),
        name="winds",
    )(spec, table, pairing, basis, eta, cells)
    adv, disp = pl.pallas_call(
        hand_over,
        out_shape=(
            jax.ShapeDtypeStruct(adv.shape, adv.dtype),
            jax.ShapeDtypeStruct(disp.shape, disp.dtype),
        ),
        in_specs=[anywhere] * 2,
        out_specs=(anywhere, anywhere),
        scratch_shapes=[
            pltpu.VMEM(adv.shape, adv.dtype),
            pltpu.VMEM(disp.shape, disp.dtype),
            dma((2, 2, 2)),
            dma((2, 2, 2)),
        ],
        name="results",
    )(adv, disp)
    whole = lambda a: jnp.swapaxes(a, -3, -2).reshape(2, 2, 8, lon_total)
    return whole(adv), whole(disp.reshape(2, 2, nq, 8, 128))


def solution(mesh):
    return jax.shard_map(
        per_device,
        mesh=mesh,
        in_specs=(
            P(None, "lev", "band", None),
            P("lev", None, "band", None),
            P("band"),
            P("lev", "band", None),
            P(None, "lev", "band", None),
        ),
        out_specs=(P(None, "lev", "band", None), P(None, "lev", "band", None)),
        check_vma=False,
    )
```

```python
import functools
import math

import jax
import jax.numpy as jnp
import numpy as np
from jax import lax
from jax.experimental import pallas as pl
from jax.experimental.pallas import tpu as pltpu
from jax.sharding import PartitionSpec as P

ITERS = 2
COURANT = 0.8
MESH = pl.DeviceIdType.MESH
BF16 = jnp.bfloat16
F32 = jnp.float32
TAP = jnp.bfloat16
VMEM_LIMIT = 60 * 1024 * 1024
GROUPS = 16


def nt_dot(a, b):
    return lax.dot_general(a, b, (((1,), (1,)), ((), ())), preferred_element_type=F32)


def tn_dot(a, b):
    return lax.dot_general(a, b, (((0,), (0,)), ((), ())), preferred_element_type=F32)


def gather_sums(
    nb,
    nx,
    pairs,
    width,
    after_sums,
    after_sends,
    after_own,
    spec_ref,
    leg_ref,
    pair_ref,
    recv,
    halo,
    raw,
    specg,
    last,
    legs,
    sums_out,
    sums_in,
    stage,
    send,
    load_sem,
    last_send,
    last_recv,
    spec_send,
    spec_recv,
    leg_send,
    leg_recv,
    x_send,
    x_recv,
    band_send,
    band_recv,
    halo_send,
    halo_recv,
    lev_ready,
    band_ready,
):
    b = lax.axis_index("band")
    lev = lax.axis_index("lev")
    nlev = 2 * nx
    x = lev // 2
    core = lev % 2
    group = max(1, nb // GROUPS)

    def remote(src, dst, send_sem, recv_sem, band, level):
        return pltpu.make_async_remote_copy(
            src_ref=src,
            dst_ref=dst,
            send_sem=send_sem,
            recv_sem=recv_sem,
            device_id=(band, level),
            device_id_type=MESH,
        )

    def signal(semaphore, band, level):
        pl.semaphore_signal(semaphore, inc=1, device_id=(band, level), device_id_type=MESH)

    side = math.isqrt(nb)

    def hops(d):
        return sum(min(n, side - n) for n in (d // side, d % side))

    order = sorted(range(1, nb), key=lambda d: -hops(d))
    sibling = (b, 2 * x + 1 - core)

    loads = (
        pltpu.make_async_copy(spec_ref, raw, load_sem.at[0]),
        pltpu.make_async_copy(leg_ref, legs.at[:, core], load_sem.at[1]),
    )
    for load in loads:
        load.start()
    barrier = pltpu.get_barrier_semaphore()

    for d in range(1, nx):
        signal(barrier, b, 2 * lax.rem(x + d, nx))

    @pl.when(core == 1)
    def _():
        signal(barrier, b, 2 * x)

    for d in order:
        signal(barrier, lax.rem(b + d, nb), 2 * x + 1)
    loads[0].wait()
    tail = jnp.zeros((16, 128), F32)
    place = lax.broadcasted_iota(jnp.int32, (16, 128), 1)
    for p in range(pairs):
        own = jnp.concatenate([raw[0, p], raw[1, p]], axis=0)
        specg[p, 0] = own[:, : width - 1]
        tail = jnp.where(place == p, own[:, width - 1 :].astype(F32), tail)
    last[0] = tail.astype(BF16)

    @pl.when(core == 0)
    def _():
        pl.semaphore_wait(barrier, nlev - 1)
        signal(lev_ready, *sibling)

    @pl.when(core == 1)
    def _():
        pl.semaphore_wait(lev_ready, 1)

    for p in range(pairs):
        for d in sorted(range(1, nx), key=lambda d: -min(d, nx - d)):
            target = 2 * lax.rem(x + d, nx) + core
            if p == 0:
                remote(last.at[0], last.at[d], last_send, last_recv, b, target).start()
            remote(specg.at[p, 0], specg.at[p, d], spec_send, spec_recv.at[p], b, target).start()
        if p == 0:
            loads[1].wait()
        remote(legs.at[p, core], legs.at[p, core], leg_send, leg_recv.at[p], *sibling).start()

    after_sums()

    columns = lax.broadcasted_iota(jnp.int32, (16, width - 1), 1)
    zero = jnp.zeros((16, width - 1), F32)
    no_tail = jnp.zeros((16, 1), F32)
    others = last.at[pl.ds(1, nx - 1)]
    remote(others, others, last_send, last_recv, *sibling).wait_recv()
    for p in range(pairs):
        others = specg.at[p, pl.ds(1, nx - 1)]
        remote(others, others, spec_send, spec_recv.at[p], *sibling).wait_recv()
        table_ref = legs.at[p, 0]
        remote(table_ref, table_ref, leg_send, leg_recv.at[p], *sibling).wait_recv()
        first_part = columns < (width - 1 - pair_ref[p])
        parts = []
        for d in range(nx):
            values = specg[p, d].astype(F32)
            tail = last[d].astype(F32)[:, p : p + 1]
            parts.append(jnp.concatenate([jnp.where(first_part, values, zero), no_tail], axis=1))
            parts.append(jnp.concatenate([jnp.where(first_part, zero, values), tail], axis=1))
        rows = jnp.concatenate(parts, axis=0).astype(BF16)
        table = jnp.concatenate([legs[p, 0], legs[p, 1]], axis=0)
        total = nt_dot(rows, table).astype(BF16)
        for d in range(nx):
            sums_out[p, d] = total[d * 32 : (d + 1) * 32]
        sums_in[p, x] = total[:32]
        for d in range(nx - 1, 0, -1):
            remote(
                sums_out.at[p, d],
                sums_in.at[p, x],
                x_send,
                x_recv.at[p],
                b,
                2 * lax.rem(x + nx - d, nx) + core,
            ).start()

    lanes = nx * 32
    lane = lax.broadcasted_iota(jnp.int32, (nb, lanes), 1)
    band = lax.broadcasted_iota(jnp.int32, (nb, lanes), 0)
    numbers = jnp.zeros((nb, lanes), jnp.int32)
    for p in range(pairs):
        numbers = jnp.where(lane == 2 * p, pair_ref[p] // 128, numbers)
        numbers = jnp.where(lane == 2 * p + 1, pair_ref[p] % 128, numbers)
    stage[pl.ds(3 * pairs, nb, stride=16), :] = numbers.astype(F32)
    square = (2 * nb, 2 * nb)
    unit = jnp.where(
        lax.broadcasted_iota(jnp.int32, square, 0) == lax.broadcasted_iota(jnp.int32, square, 1),
        1.0,
        0.0,
    ).astype(BF16)
    before = (lane // 32) % 2 == 0
    outside = ((band == 0) & before) | ((band == nb - 1) & jnp.logical_not(before))
    for p in range(pairs):
        others = sums_out.at[p, pl.ds(1, nx - 1)]
        remote(others, others, x_send, x_recv.at[p], *sibling).wait_recv()
        block = jnp.concatenate([sums_in[p, other] for other in range(nx)], axis=0)
        turned = nt_dot(unit, block)
        low, high = turned[:nb], turned[nb:]
        stage[pl.ds(2 * p, nb, stride=16), :] = low
        stage[pl.ds(2 * p + 1, nb, stride=16), :] = high
        edge = jnp.where(lane < 64, pltpu.roll(low, 32, 1), pltpu.roll(high, 96, 1))
        edge = jnp.where(before, pltpu.roll(edge, 1, 0), pltpu.roll(edge, nb - 1, 0))
        edge = jnp.where(outside, 0.0, edge)
        stage[pl.ds(2 * pairs + p, nb, stride=16), :] = edge
    send[...] = stage[...].reshape(nb, 16, lanes).astype(BF16)
    recv[nb - 1] = send[b]

    @pl.when(core == 1)
    def _():
        pl.semaphore_wait(barrier, 2 * (nb - 1))
        signal(band_ready, *sibling)

    @pl.when(core == 0)
    def _():
        pl.semaphore_wait(band_ready, 1)

    for n, d in enumerate(order):
        target = lax.rem(b + d, nb)
        remote(
            send.at[target], recv.at[n], band_send, band_recv.at[n // group], target, lev
        ).start()

    above = (b, lax.rem(lev + 1, nlev))
    below = (b, lax.rem(lev + nlev - 1, nlev))

    @pl.when(lev == 0)
    def _():
        halo[0] = jnp.zeros(recv.shape, BF16)

    @pl.when(lev == nlev - 1)
    def _():
        halo[1] = jnp.zeros(recv.shape, BF16)

    after_sends()
    for g in reversed(range(GROUPS)):
        end = min(nb - 1, (g + 1) * group)
        if end > g * group:
            arrived = recv.at[pl.ds(g * group, end - g * group)]
            remote(arrived, arrived, band_send, band_recv.at[g], *sibling).wait_recv()
        part = pl.ds(g * group, group)

        @pl.when(lev < nlev - 1)
        def _():
            remote(
                recv.at[part], halo.at[0, part], halo_send.at[0], halo_recv.at[0], *above
            ).start()

        @pl.when(lev > 0)
        def _():
            remote(
                recv.at[part], halo.at[1, part], halo_send.at[1], halo_recv.at[1], *below
            ).start()

    after_own()
    others = last.at[pl.ds(1, nx - 1)]
    remote(others, others, last_send, last_recv, *sibling).wait_send()
    others = specg.at[:, pl.ds(1, nx - 1)]
    remote(others, others, spec_send, spec_recv.at[0], *sibling).wait_send()
    tables = legs.at[:, 0]
    remote(tables, tables, leg_send, leg_recv.at[0], *sibling).wait_send()
    others = sums_out.at[:, pl.ds(1, nx - 1)]
    remote(others, others, x_send, x_recv.at[0], *sibling).wait_send()
    arrived = recv.at[pl.ds(0, nb - 1)]
    remote(arrived, arrived, band_send, band_recv.at[0], *sibling).wait_send()

    up = remote(recv, halo.at[0], halo_send.at[0], halo_recv.at[0], *above)
    down = remote(recv, halo.at[1], halo_send.at[1], halo_recv.at[1], *below)

    @pl.when(lev > 0)
    def _():
        up.wait_recv()
        down.wait_send()

    @pl.when(lev < nlev - 1)
    def _():
        down.wait_recv()
        up.wait_send()


def lagrange_taps(shift, back):
    here = back == 0.0
    x = jnp.clip(back - shift, -0.5, 1.5)
    xm1, xm2, xp1 = x - 1.0, x - 2.0, x + 1.0
    tail = xm1 * xm2
    head = xp1 * x
    first = x * tail * (-1.0 / 6.0)
    second = xp1 * tail * 0.5
    third = head * xm2 * -0.5
    fourth = head * xm1 * (1.0 / 6.0)
    return (
        jnp.where(here, 0.0, first),
        jnp.where(here, first, second),
        jnp.where(here, second, third),
        jnp.where(here, third, fourth),
        jnp.where(here, fourth, 0.0),
    )


def weighted(taps, values):
    total = taps[0] * values[0]
    for tap, value in zip(taps[1:], values[1:]):
        total = total + tap * value
    return total


def whole_kernel(
    nb,
    nx,
    nq,
    pairs,
    width,
    spec_ref,
    leg_ref,
    pair_ref,
    basis_ref,
    eta_ref,
    cells_ref,
    adv_ref,
    disp_ref,
    wide,
    slots,
    place,
    orders,
    coef,
    basis,
    grid,
    near,
    eta,
    cells,
    points,
    eta_wide,
    disp,
    adv_wide,
    adv,
    basis_sem,
    point_sem,
    out_sem,
    recv,
    halo,
    *rest,
):
    qp = grid.shape[0] // 289
    half = nb * pairs // 2
    window = place.shape[1] // 2
    lon_half = nq * 64
    units = qp // 8
    rows = 8
    row0 = lax.axis_index("band") * rows
    lev0 = lax.axis_index("lev") * 2

    blocks = [(start, min(256, lon_half - start)) for start in range(0, lon_half, 256)]
    basis_copies = [
        pltpu.make_async_copy(
            basis_ref.at[:, :, pl.ds(start, size)],
            basis.at[:, :, pl.ds(start, size)],
            basis_sem.at[n],
        )
        for n, (start, size) in enumerate(blocks)
    ]
    point_copies = (
        pltpu.make_async_copy(eta_ref, eta, point_sem.at[0]),
        pltpu.make_async_copy(cells_ref, cells, point_sem.at[1]),
    )

    def start_copies():
        for copy in (*point_copies, *basis_copies):
            copy.start()

    def read_points():
        for copy in (*point_copies, *basis_copies):
            copy.wait()
        lon = (
            lax.broadcasted_iota(jnp.int32, (nq, 128), 0) * 128
            + lax.broadcasted_iota(jnp.int32, (nq, 128), 1)
        )
        for k in range(2):
            eta_wide[...] = eta[k].astype(F32).reshape(nq * 8, 128)
            for i in range(rows):
                part = pl.ds(i, nq, stride=8)
                at = pl.ds(k * qp, nq)
                points[i, 0, at, :] = jnp.where(cells[0, k, part, :] == row0 + i, 0.0, 1.0)
                points[i, 1, at, :] = jnp.where(cells[1, k, part, :] == lon, 0.0, 1.0)
                points[i, 2, at, :] = jnp.where(cells[2, k, part, :] == lev0 + k, 0.0, 1.0)
                points[i, 3, at, :] = eta_wide[part, :]

    lane = lax.broadcasted_iota(jnp.int32, (16, 128), 1).astype(F32).astype(TAP)
    inside = {c: (lane >= c if c > 0 else lane < 128 + c) for c in (-2, -1, 1, 2)}

    def shift_fields(first, count, n, carry):
        row, level = n // count, first + n % count
        if count == 4:
            level = level + 2 * (n % count // 2)
        at = (row * 6 + level) * 4
        for two in range(2):
            for t in range(units):

                def block(offset):
                    return jnp.concatenate(
                        [
                            grid[pl.ds((at + field) * qp + 8 * t + offset, 8), :]
                            for field in (2 * two, 2 * two + 1)
                        ],
                        axis=0,
                    ).astype(TAP)

                ahead, here, after = block(0), block(1), block(2)
                for c in range(-2, 3):
                    value = here
                    if c > 0:
                        value = pltpu.roll(jnp.where(inside[c], here, after), 128 - c, 1)
                    elif c < 0:
                        value = pltpu.roll(jnp.where(inside[c], here, ahead), -c, 1)
                    near[row, level, t, two, c + 2] = value
        return carry

    def synthesise(groups, place_of, sums_of):
        first, count = place_of[groups[0]], len(groups)
        for g in groups:
            wide[...] = sums_of[g].astype(F32).reshape(nb * 16, 128)
            for p in range(pairs):
                for t, at in enumerate((2 * p, 2 * p + 1, 2 * pairs + p)):
                    lanes = (place_of[g] * 3 + t) * 128
                    slots[p * nb : (p + 1) * nb, lanes : lanes + 128] = wide[
                        pl.ds(at, nb, stride=16), :
                    ].astype(BF16)
            if g == 1:
                numbers = wide[pl.ds(3 * pairs, nb, stride=16), :].astype(jnp.int32)
                column = lax.broadcasted_iota(jnp.int32, (nb, 2 * window), 1)
                order = jnp.where(column < window, 2 * column, 2 * (column - window) + 1)
                for p in range(pairs):
                    number = (
                        numbers[:, 2 * p : 2 * p + 1] * 128 + numbers[:, 2 * p + 1 : 2 * p + 2]
                    )
                    place[p * nb : (p + 1) * nb, :] = jnp.where(order == number, 1.0, 0.0).astype(
                        BF16
                    )
        used = slots[:, first * 384 : (first + count) * 384]
        orders[first * 48 : (first + count) * 48] = tn_dot(used, place[...]).reshape(
            count * 48, 8, 2 * window
        )
        lines = pl.ds(first * 96, count * 96)
        for parity in range(2):
            for part in range(4):
                start = window * ((part // 2 + parity) % 2)
                coef[parity, part, lines, :] = jnp.concatenate(
                    [
                        orders[first * 48 + 4 * m + part, :, start : start + window]
                        for m in range(12 * count)
                    ],
                    axis=0,
                ).astype(BF16)
        for start, size in blocks:
            even, odd = [
                sum(
                    jnp.dot(
                        coef[parity, part, lines, :half],
                        basis[parity, part * half : (part + 1) * half, start : start + size],
                        preferred_element_type=F32,
                    )
                    for part in range(4)
                )
                for parity in range(2)
            ]
            for turn, values in enumerate((even + odd, even - odd)):
                for m in range(12 * count):
                    g, t, xs = groups[m // 12], (m // 4) % 3, m % 4
                    row = 2 + 2 * xs + t if t < 2 else (xs // 2 + (xs % 2) * 10)
                    base = (row * 3 + g) * 8 * qp + 1 + (start + turn * lon_half) // 128
                    for w in range(size // 128):
                        grid[pl.ds(base + w, 8, stride=qp), :] = values[
                            m * 8 : (m + 1) * 8, w * 128 : (w + 1) * 128
                        ]
        for row in range(12):
            for g in groups:
                base = (row * 3 + g) * 8 * qp
                for target, source in ((0, nq), (nq + 1, 1)):
                    grid[pl.ds(base + target, 8, stride=qp), :] = grid[
                        pl.ds(base + source, 8, stride=qp), :
                    ]
        shift = functools.partial(shift_fields, 2 * groups[0], 2 * count)
        lax.fori_loop(0, 24 * count, shift, 0, unroll=12)

    place_of = (1, 0, 2)

    def own_levels():
        synthesise((1,), place_of, {1: recv[...]})

    gather_sums(
        nb,
        nx,
        pairs,
        width,
        start_copies,
        read_points,
        own_levels,
        spec_ref,
        leg_ref,
        pair_ref,
        recv,
        halo,
        *rest,
    )
    synthesise((0, 2), place_of, {0: halo[0], 2: halo[1]})
    def double(taps):
        return [jnp.concatenate([tap, tap], axis=0).astype(TAP) for tap in taps]

    def depart(k, t, i, carry):
        at = pl.ds(pl.multiple_of((k * units + t) * 8, 8), 8)
        row_back, lon_back = points[i, 0, at, :], points[i, 1, at, :]
        level_taps = double(lagrange_taps(points[i, 3, at, :], points[i, 2, at, :]))

        def level_sums(two):
            return [
                [
                    weighted(level_taps, [near[i + b, k + a, t, two, c] for a in range(5)])
                    for c in range(5)
                ]
                for b in range(5)
            ]

        def horizontal(sums, shift_row, shift_lon):
            row_taps = lagrange_taps(shift_row, row_back)
            lon_taps = double(lagrange_taps(shift_lon, lon_back))
            lines = [weighted(lon_taps, sums[b]).astype(F32) for b in range(5)]
            return [
                weighted(row_taps, [line[s * 8 : (s + 1) * 8] for line in lines]) for s in range(2)
            ]

        wind = near[i + 2, k + 2, t, 0, 2].astype(F32)
        east, north = wind[:8], wind[8:]
        wind_sums = level_sums(0)
        shift_row, shift_lon = COURANT * north, COURANT * east
        for sweep in range(ITERS):
            east_found, north_found = horizontal(wind_sums, shift_row, shift_lon)
            shift_row = 0.5 * COURANT * (north + north_found)
            shift_lon = 0.5 * COURANT * (east + east_found)
        heat, moisture = horizontal(level_sums(1), shift_row, shift_lon)
        out = pl.ds(t * 64 + i, 8, stride=8)
        disp[0, k, out, :] = shift_row
        disp[1, k, out, :] = shift_lon
        adv_wide[0, k, out, :] = heat
        adv_wide[1, k, out, :] = moisture
        return carry

    def results(k, t, size):
        for which in range(2):
            blocks = pl.ds(t * 8, size)
            lines = pl.ds(pl.multiple_of(t * 64, 64), size * 8)
            adv[which, k, blocks] = (
                adv_wide[which, k, lines, :].reshape(size, 8, 128).astype(BF16)
            )
            pltpu.make_async_copy(
                adv.at[which, k, blocks], adv_ref.at[which, k, blocks], out_sem.at[0]
            ).start()
            pltpu.make_async_copy(
                disp.at[which, k, lines], disp_ref.at[which, k, lines], out_sem.at[1]
            ).start()

    def depart_block(n, carry):
        k, t = n // units, n % units
        lax.fori_loop(0, rows, functools.partial(depart, k, t), 0, unroll=8)

        @pl.when(t < units - 1)
        def _():
            results(k, t, 8)

        @pl.when(t == units - 1)
        def _():
            results(k, t, nq - 8 * (units - 1))

        return carry

    lax.fori_loop(0, 2 * units, depart_block, 0)
    pltpu.make_async_copy(adv.at[:, :, pl.ds(0, nq)], adv_ref, out_sem.at[0]).wait()
    pltpu.make_async_copy(disp.at[:, :, pl.ds(0, nq * 8)], disp_ref, out_sem.at[1]).wait()


def basis_table(total, lon_total):
    npairs = total // 2
    m = np.arange(npairs // 2, dtype=np.int64)
    j = np.arange(lon_total // 2, dtype=np.int64)
    orders = ((2 * m, total - 2 - 2 * m), (2 * m + 1, total - 1 - 2 * m))
    table = np.zeros((2, 2, 2, npairs // 2, lon_total // 2), np.float32)
    for parity in range(2):
        for half in range(2):
            order = orders[parity][half][:, None]
            angle = (2.0 * math.pi / lon_total) * ((order * j[None, :]) % lon_total)
            weight = np.where(order == 0, 1.0, 2.0)
            table[parity, half, 0] = weight * np.cos(angle)
            table[parity, half, 1] = -weight * np.sin(angle)
    return jnp.asarray(table.reshape(2, 2 * npairs, lon_total // 2).astype(BF16))


def hand_over(adv_ref, disp_ref, adv_out, disp_out, adv, disp, in_sem, out_sem):
    steps = []
    for n, (source, held, target) in enumerate(
        ((disp_ref, disp, disp_out), (adv_ref, adv, adv_out))
    ):
        for which in range(2):
            for k in range(2):
                at = (n, which, k)
                inward = pltpu.make_async_copy(
                    source.at[which, k], held.at[which, k], in_sem.at[at]
                )
                outward = pltpu.make_async_copy(
                    held.at[which, k], target.at[which, k], out_sem.at[at]
                )
                inward.start()
                steps.append((inward, outward))
    for inward, outward in steps:
        inward.wait()
        outward.start()
    for inward, outward in steps:
        outward.wait()


def per_device(spectra, legendre, pairing, eta_shift, cells):
    nb = legendre.shape[1]
    pairs, width = spectra.shape[2], spectra.shape[3]
    nx = lax.axis_size("lev") // 2
    lon_total = eta_shift.shape[2]
    nq = lon_total // 128
    qp = -(-(nq + 2) // 8) * 8
    basis = basis_table(width - 1, lon_total)
    window = -(-(width - 1) // 4 // 128) * 128
    tiles = lambda a: jnp.swapaxes(a.reshape(a.shape[:-1] + (nq, 128)), -3, -2)
    eta = tiles(eta_shift)
    cells = tiles(cells).reshape(3, 2, nq * 8, 128)
    spec = jnp.transpose(spectra, (0, 2, 1, 3))
    table = jnp.transpose(legendre[0], (1, 0, 2))
    lanes = nx * 32
    dma = pltpu.SemaphoreType.DMA
    regular = pltpu.SemaphoreType.REGULAR
    anywhere = pl.BlockSpec(memory_space=pl.ANY)
    adv, disp = pl.pallas_call(
        functools.partial(whole_kernel, nb, nx, nq, pairs, width),
        out_shape=(
            jax.ShapeDtypeStruct((2, 2, nq, 8, 128), BF16),
            jax.ShapeDtypeStruct((2, 2, nq * 8, 128), F32),
        ),
        in_specs=[anywhere, anywhere, pl.BlockSpec(memory_space=pltpu.SMEM)] + [anywhere] * 3,
        out_specs=(anywhere, anywhere),
        scratch_shapes=[
            pltpu.VMEM((nb * 16, 128), F32),
            pltpu.VMEM((nb * pairs, 9 * 128), BF16),
            pltpu.VMEM((nb * pairs, 2 * window), BF16),
            pltpu.VMEM((144, 8, 2 * window), F32),
            pltpu.VMEM((2, 4, 288, window), BF16),
            pltpu.VMEM(basis.shape, BF16),
            pltpu.VMEM((289 * qp, 128), F32),
            pltpu.VMEM((12, 6, qp // 8, 2, 5, 16, 128), TAP),
            pltpu.VMEM(eta.shape, BF16),
            pltpu.VMEM(cells.shape, jnp.int32),
            pltpu.VMEM((8, 4, 2 * qp, 128), F32),
            pltpu.VMEM((nq * 8, 128), F32),
            pltpu.VMEM((2, 2, qp * 8 + 8, 128), F32),
            pltpu.VMEM((2, 2, qp * 8 + 8, 128), F32),
            pltpu.VMEM((2, 2, qp, 8, 128), BF16),
            dma((-(-lon_total // 512),)),
            dma((2,)),
            dma((2,)),
            pltpu.VMEM((nb, 16, lanes), BF16),
            pltpu.VMEM((2, nb, 16, lanes), BF16),
            pltpu.VMEM(spec.shape, BF16),
            pltpu.VMEM((pairs, nx, 16, width - 1), BF16),
            pltpu.VMEM((nx, 16, 128), BF16),
            pltpu.VMEM((pairs, 2, nb, width), BF16),
            pltpu.VMEM((pairs, nx, 32, 2 * nb), BF16),
            pltpu.VMEM((pairs, nx, 32, 2 * nb), BF16),
            pltpu.VMEM((nb * 16, lanes), F32),
            pltpu.VMEM((nb, 16, lanes), BF16),
            dma((2,)),
            dma,
            dma,
            dma,
            dma((pairs,)),
            dma,
            dma((pairs,)),
            dma,
            dma((pairs,)),
            dma,
            dma((GROUPS,)),
            dma((2,)),
            dma((2,)),
            regular,
            regular,
        ],
        compiler_params=pltpu.CompilerParams(
            collective_id=0, has_side_effects=True, vmem_limit_bytes=VMEM_LIMIT
        ),
        name="winds",
    )(spec, table, pairing, basis, eta, cells)
    adv, disp = pl.pallas_call(
        hand_over,
        out_shape=(
            jax.ShapeDtypeStruct(adv.shape, adv.dtype),
            jax.ShapeDtypeStruct(disp.shape, disp.dtype),
        ),
        in_specs=[anywhere] * 2,
        out_specs=(anywhere, anywhere),
        scratch_shapes=[
            pltpu.VMEM(adv.shape, adv.dtype),
            pltpu.VMEM(disp.shape, disp.dtype),
            dma((2, 2, 2)),
            dma((2, 2, 2)),
        ],
        name="results",
    )(adv, disp)
    whole = lambda a: jnp.swapaxes(a, -3, -2).reshape(2, 2, 8, lon_total)
    return whole(adv), whole(disp.reshape(2, 2, nq, 8, 128))


def solution(mesh):
    return jax.shard_map(
        per_device,
        mesh=mesh,
        in_specs=(
            P(None, "lev", "band", None),
            P("lev", None, "band", None),
            P("band"),
            P("lev", "band", None),
            P(None, "lev", "band", None),
        ),
        out_specs=(P(None, "lev", "band", None), P(None, "lev", "band", None)),
        check_vma=False,
    )
```
